256 devices in a mesh: shard: 64 (over z, x, core), sub: 4 (over y).
Axes of the slice: x: 4, y: 4, z: 8, core: 2. Of those that a mesh axis runs over, the one named last changes fastest.
Arguments:
- feats: bfloat16 [8192, 4096], P(('shard', 'sub')), may hold values from -24 to 24
- w_hidden: bfloat16 [4096, 4096], P(None, 'sub'), may hold values from -0.09375 to 0.09375
- w_embed: bfloat16 [4096, 256], P('sub'), may hold values from -0.09375 to 0.09375
- items: bfloat16 [262144, 256], P(('shard', 'sub')), may hold values from -0.5 to 0.5
- teacher: bfloat16 [65536, 128], P(('shard', 'sub')), may hold values from -6 to 6
- block_counts: int32 [256, 32], P(('shard', 'sub')), may hold values from 1 to 32, 256 in all within a row
- tail_rows: int32 [8192], P(('shard', 'sub')), may hold values from 1 to 128
- cand_owner: int32 [65536, 1], P(('shard', 'sub')), may hold values from 0 to 255; in each aligned block of 256 rows (0 to 255, 256 to 511, ...) at most 2 rows name the same one
- cand_block: int32 [65536], P(('shard', 'sub')), may hold values from 0 to 7
Outputs:
- grad_feats: float32 [8192, 4096], P(('shard', 'sub'))
- grad_hidden: float32 [4096, 4096], P('shard', 'sub')
- grad_embed: float32 [4096, 256], P('sub')
- grad_items: float32 [262144, 256], P(('shard', 'sub'))
The draws below stay inside these ranges and needn't reach their ends.
Inputs may be any that keep to these rules, and one draw needn't show every extreme that they name: `block_counts`: each device's row sums to 256; one count in each row is exactly 32. `cand_owner`: among the rows of one device no owner appears more than 2 times; some owner appears exactly 2 times in some device's rows.
All inputs are finite; a program needn't handle non-finite values.
Results may differ from the reference program's by a relative error of at most 0.013.
Values may be sent and summed in bfloat16 or wider, within the bound.
A program may use at most 128 MiB of HBM per device.

```python
import math
import jax
import jax.numpy as jnp
import numpy as np
from jax import lax

D = 4096
EMBED_WIDTH = 256
BLK = 128
MOSTB = 32
QUERIES_PER_UNIT = 32
BLK_DEV = 8
SLOT_DEV = 256
CAP = 2
QUERIES = 8192
SLOTS = 65536
ITEMS = 262144
DEVICES = 256


def set_ends(result, own_key, smallest, high):
    spot = [jax.random.randint(jax.random.fold_in(own_key, axis), (), 0, length) for axis, length in enumerate(result.shape)]
    longest = result.shape.index(max(result.shape))
    next_to = spot[:longest] + [(spot[longest] + 1) % result.shape[longest]] + spot[longest + 1:]
    return result.at[tuple(spot)].set(smallest).at[tuple(next_to)].set(high)


def spiked(array, stream_key, source, target, parts, factor):
    def block_of(dim):
        return (jnp.arange(array.shape[dim]) // (array.shape[dim] // parts)).reshape((-1,) + (1,) * (array.ndim - 1 - dim))

    near = jax.random.permutation(stream_key, parts)[block_of(target)]
    second = (block_of(target) + parts // 2) % parts
    return jnp.where((block_of(source) == near) | (block_of(source) == second), factor * array, array)


def steps_of(key, extent, pieces, least, high):
    level, own = 1.0, jax.random.fold_in(key, 6)
    for position, parts in pieces:
        steps = jnp.exp(jax.random.uniform(jax.random.fold_in(own, position), (parts,), jnp.float32, least / len(pieces), high / len(pieces)))
        level = level * jnp.repeat(steps, extent[position] // parts).reshape([-1 if axis == position else 1 for axis in range(len(extent))])
    return level


def profile(count, total, reach, slope):
    loads = [(1 << 20) // math.isqrt(standing ** slope) + 1 for standing in range(2, count + 1)]
    surplus, counts = total - reach - (count - 1), [1] * (count - 1)
    while surplus > 0:
        free = [i for i in range(count - 1) if counts[i] < reach]
        pool, remaining = sum([loads[i] for i in free]), surplus
        for i in free:
            extra = min(reach - counts[i], max(1, remaining * loads[i] // pool), surplus)
            counts[i] = counts[i] + extra
            surplus = surplus - extra
    return np.array([reach] + counts)


def uneven_parts(stream_key, number_of, total, reach, lean):
    if number_of == 2:
        one = jax.random.randint(stream_key, (), max(1, total - reach), min(reach, total - 1) + 1)
        return jnp.stack([one, total - one])
    lengths = jnp.asarray(profile(number_of, total, reach, lean), jnp.int32)
    twos = (number_of - 1) // 2
    giver, receiver = lengths[1:1 + 2 * twos:2], lengths[2:2 + 2 * twos:2]
    room = jnp.minimum(giver - 1, reach - receiver)
    shifted = jax.random.randint(jax.random.fold_in(stream_key, 1), (twos,), 0, 1 << 20) % (room + 1)
    lengths = lengths.at[1:1 + 2 * twos:2].set(giver - shifted).at[2:2 + 2 * twos:2].set(receiver + shifted)
    return lengths[jax.random.permutation(jax.random.fold_in(stream_key, 2), number_of)]


def routed_block(stream_key, own, number, rows, number_of, top, limit, skew):
    order = jax.random.permutation(stream_key, number_of)
    heavy_load, usual = shares(number_of, rows * top, limit, skew, True), shares(number_of, rows * top, limit, skew, False)
    places = jnp.arange(number_of)

    def named(tallies, rotation):
        used = int((tallies > 0).sum())
        fixed = max(1, used // 4)
        moved = fixed + (places - fixed + rotation * (used - fixed)) % max(1, number_of - fixed)
        return jnp.zeros((number_of,), jnp.int32).at[order[jnp.where(places < fixed, places, moved)]].set(jnp.asarray(tallies, jnp.int32))

    tallies = jnp.where(number % 4 == 0, named(heavy_load, number // 4), named(usual, number - number // 4 - 1))
    mixed = jax.random.permutation(jax.random.fold_in(own, 3), number_of)
    donor, sink = mixed[0:number_of // 2 * 2:2], mixed[1:number_of // 2 * 2:2]
    slack = jnp.minimum(tallies[donor] - 1, limit - tallies[sink]) // 2
    slack = jnp.where((donor == order[0]) | (sink == order[0]) | (tallies[sink] == 0), 0, jnp.maximum(slack, 0))
    moved = jax.random.randint(jax.random.fold_in(own, 4), (number_of // 2,), 0, 1 << 20) % (slack + 1)
    tallies = tallies.at[donor].add(-moved).at[sink].add(moved)
    labels = jnp.searchsorted(jnp.cumsum(tallies), jnp.arange(rows * top), side="right").astype(jnp.int32)
    listing = labels.reshape(top, rows).T
    listing = listing[jax.random.permutation(jax.random.fold_in(own, 1), rows)]
    rotation = jax.random.randint(jax.random.fold_in(own, 2), (rows, 1), 0, top)
    return jnp.take_along_axis(listing, (jnp.arange(top)[None, :] + rotation) % top, axis=1)


def shares(amount, total, bound, slope, full):
    weights = [(1 << 20) // math.isqrt(grade ** slope) + 1 for grade in range(1, amount + 1)]
    largest = bound if full else min(bound, max(-(-total // amount), total * weights[0] // sum(weights)))
    least = 1 if total - largest >= amount - 1 else 0
    given, spare = [largest] + [least] * (amount - 1), total - largest - least * (amount - 1)
    while spare > 0:
        free = [i for i in range(1, amount) if given[i] < largest] or [i for i in range(1, amount) if given[i] < bound]
        pool, remaining = sum([weights[i] for i in free]), spare
        for i in free:
            addition = min(bound - given[i], max(1, remaining * weights[i] // pool), spare)
            given[i] = given[i] + addition
            spare = spare - addition
    return np.array(given)


def centred(stream_key, shape, scale, limit, shards=(), kind=jnp.bfloat16):
    array = jax.random.normal(stream_key, shape, jnp.float32) * scale
    if len(shards) > 0:
        array = steps_of(stream_key, shape, shards, -0.22, 0.18) * array
    return jnp.clip(array, min=-limit, max=limit).astype(kind)


def heavy_noise(own_key, shape, width, bound, cuts, heavy, kind=jnp.bfloat16):
    result = width * jax.random.normal(own_key, shape, jnp.float32)
    if cuts:
        result = result * steps_of(own_key, shape, cuts, -0.22, 0.18)
    return jnp.clip(spiked(result, jax.random.fold_in(own_key, 3), *heavy), -bound, bound).astype(kind)


def setup_inputs(seed: int = 0) -> dict:
    key_list = jax.random.split(jax.random.key(seed), 10)
    feats = heavy_noise(key_list[0], (QUERIES, D), 1.0, 24.0, ((0, 256),), (0, 1, 256, 6.0))
    w_hidden = centred(key_list[1], (D, D), D ** -0.5, 0.09375, ((1, 4),))
    w_embed = centred(key_list[2], (D, EMBED_WIDTH), D ** -0.5, 0.09375, ((0, 4),))
    items = centred(key_list[3], (ITEMS, EMBED_WIDTH), 0.0625, 0.5, ((0, 256),))
    teacher = centred(key_list[4], (SLOTS, BLK), 1.0, 6.0, ((0, 256),))
    block_counts = jax.vmap(lambda own: uneven_parts(own, QUERIES_PER_UNIT, SLOT_DEV, MOSTB, 2))(jax.random.split(key_list[5], DEVICES)).reshape((DEVICES, QUERIES_PER_UNIT)).astype(jnp.int32)
    tail_rows = set_ends(jax.random.randint(key_list[6], (QUERIES,), 1, BLK + 1), jax.random.fold_in(key_list[6], 1), 1, BLK).astype(jnp.int32)
    cand_owner_keys = jax.random.split(jax.random.fold_in(key_list[7], 1), SLOTS // SLOT_DEV)
    cand_owner_turns = jax.random.permutation(jax.random.fold_in(key_list[7], 3), SLOTS // SLOT_DEV)
    cand_owner = jax.vmap(lambda own, number: routed_block(jax.random.fold_in(key_list[7], 2), own, number, SLOT_DEV, DEVICES, 1, CAP, 2))(cand_owner_keys, cand_owner_turns).reshape((SLOTS, 1))
    cand_block = set_ends(jax.random.randint(key_list[8], (SLOTS,), 0, BLK_DEV), jax.random.fold_in(key_list[8], 1), 0, BLK_DEV - 1).astype(jnp.int32)
    return {"feats": feats, "w_hidden": w_hidden, "w_embed": w_embed, "items": items, "teacher": teacher, "block_counts": block_counts, "tail_rows": tail_rows, "cand_owner": cand_owner, "cand_block": cand_block}


eps_norm = 1e-06

def query_softmax(logits, valid_row, group_member, local_query):
    masked = jnp.where(valid_row, logits, -jnp.inf)
    slot_top = lax.optimization_barrier(jnp.max(masked, axis=2))
    query_top = lax.optimization_barrier(jnp.max(jnp.where(group_member, slot_top[:, None, :], -jnp.inf), axis=2))
    shift_top = jnp.take_along_axis(query_top, local_query, axis=1)
    expo = jnp.where(valid_row, jnp.exp(logits - shift_top[:, :, None]), 0.0)
    slot_total = lax.optimization_barrier(jnp.sum(expo, axis=2))
    query_count_total = lax.optimization_barrier(jnp.sum(jnp.where(group_member, slot_total[:, None, :], 0.0), axis=2))
    shift_total = jnp.take_along_axis(query_count_total, local_query, axis=1)
    return expo / shift_total[:, :, None]

def reference(feats, w_hidden, w_embed, items, teacher, block_counts, tail_rows, cand_owner, cand_block):
    device_group = block_counts.shape[0]
    preact = jnp.dot(feats, w_hidden, preferred_element_type=jnp.float32)
    hidden = jax.nn.silu(preact).astype(jnp.bfloat16)
    emb_raw = jnp.dot(hidden, w_embed, preferred_element_type=jnp.float32)
    inv_rms = lax.rsqrt(lax.optimization_barrier(jnp.mean(emb_raw * emb_raw, axis=1, keepdims=True)) + eps_norm)
    query_emb = (emb_raw * inv_rms).astype(jnp.bfloat16)
    seg_ends = jnp.cumsum(block_counts, axis=1).astype(jnp.int32)
    slot_pos = jnp.arange(SLOT_DEV, dtype=jnp.int32)
    local_query = lax.optimization_barrier(jnp.sum((slot_pos[None, :, None] >= seg_ends[:, None, :]).astype(jnp.int32), axis=2)).astype(jnp.int32)
    group_member = jnp.arange(QUERIES_PER_UNIT, dtype=jnp.int32)[None, :, None] == local_query[:, None, :]
    end_of = jnp.take_along_axis(seg_ends, local_query, axis=1)
    is_last = slot_pos[None, :] == end_of - 1
    tail_dev = tail_rows.reshape(device_group, QUERIES_PER_UNIT)
    tail_fill = jnp.take_along_axis(tail_dev, local_query, axis=1)
    row_pos = jnp.arange(BLK, dtype=jnp.int32)
    valid_row = jnp.logical_or(jnp.logical_not(is_last)[:, :, None], row_pos[None, None, :] < tail_fill[:, :, None])
    query_ids = (local_query + jnp.arange(device_group, dtype=jnp.int32)[:, None] * QUERIES_PER_UNIT).astype(jnp.int32)
    gblock = (cand_owner[:, 0] * BLK_DEV + cand_block).astype(jnp.int32).reshape(device_group, SLOT_DEV)
    blocks = items.reshape(device_group * BLK_DEV, BLK, EMBED_WIDTH)
    query_slot = query_emb[query_ids.reshape(-1)].reshape(device_group, SLOT_DEV, EMBED_WIDTH)

    def score_part(inputs):
        block_ids, query_rows = inputs
        chosen = blocks[block_ids].astype(jnp.float32)
        return jnp.einsum('sre,se->sr', chosen, query_rows.astype(jnp.float32), precision=lax.Precision.HIGHEST)
    scores = lax.map(score_part, (gblock, query_slot))
    student_p = query_softmax(scores, valid_row, group_member, local_query)
    teacher_p = query_softmax(teacher.astype(jnp.float32).reshape(device_group, SLOT_DEV, BLK), valid_row, group_member, local_query)
    n_cand = ((block_counts - 1) * BLK + tail_dev).astype(jnp.float32)
    n_slot = jnp.take_along_axis(n_cand, local_query, axis=1)
    dlogit = jnp.where(valid_row, n_slot[:, :, None] * (student_p - teacher_p), 0.0)

    def grad_part(running, inputs):
        block_ids, query_rows, grad_rows = inputs
        chosen = blocks[block_ids].astype(jnp.float32)
        grad_f = grad_rows.astype(jnp.float32)
        dq_rows = jnp.einsum('sr,sre->se', grad_f, chosen, precision=lax.Precision.HIGHEST)
        contrib = grad_f[:, :, None] * query_rows.astype(jnp.float32)[:, None, :]
        running = running.at[block_ids].add(contrib)
        return (running, dq_rows)
    start_grad = jnp.zeros((device_group * BLK_DEV, BLK, EMBED_WIDTH), jnp.float32)
    item_grad, query_grad_slot = lax.scan(grad_part, start_grad, (gblock, query_slot, dlogit))
    query_gradient = jnp.einsum('crf,cfv->crv', group_member.astype(jnp.float32), query_grad_slot, precision=lax.Precision.HIGHEST).reshape(device_group * QUERIES_PER_UNIT, EMBED_WIDTH)
    grad_emb = (inv_rms * (query_gradient - emb_raw * inv_rms * inv_rms * lax.optimization_barrier(jnp.mean(query_gradient * emb_raw, axis=1, keepdims=True)))).astype(jnp.bfloat16)
    grad_embed = jnp.dot(hidden.T, grad_emb, preferred_element_type=jnp.float32)
    dhidden = jnp.dot(grad_emb, w_embed.T, preferred_element_type=jnp.float32)
    sigmoid_pre = jax.nn.sigmoid(preact)
    preact_gradient = (dhidden * sigmoid_pre * (1.0 + preact * (1.0 - sigmoid_pre))).astype(jnp.bfloat16)
    grad_hidden = jnp.dot(feats.T, preact_gradient, preferred_element_type=jnp.float32)
    grad_feats = jnp.dot(preact_gradient, w_hidden.T, preferred_element_type=jnp.float32)
    return (grad_feats, grad_hidden, grad_embed, item_grad.reshape(device_group * BLK_DEV * BLK, EMBED_WIDTH))
```

```python
import jax
import jax.numpy as jnp
from jax import lax
from jax.sharding import PartitionSpec as P

BLK = 128
BLK_DEV = 8
CAP = 2
EPS = 1e-06
HI = lax.Precision.HIGHEST
F32 = jnp.float32
BF16 = jnp.bfloat16


def dot(left, right, dims, precision=None):
    return lax.dot_general(
        left, right, ((dims[0], dims[1]), ((), ())), precision=precision, preferred_element_type=F32
    )


def nn(left, right, precision=None):
    return dot(left, right, ((1,), (0,)), precision)


def tn(left, right, precision=None):
    return dot(left, right, ((0,), (0,)), precision)


def nt(left, right, precision=None):
    return dot(left, right, ((1,), (1,)), precision)


def exchange(array):
    n_shard, n_sub = lax.axis_size("shard"), lax.axis_size("sub")
    shape = array.shape
    array = array.reshape((n_shard, n_sub, CAP) + shape[1:])
    array = lax.all_to_all(array, "shard", split_axis=0, concat_axis=0, tiled=True)
    array = lax.all_to_all(array, "sub", split_axis=1, concat_axis=1, tiled=True)
    return array.reshape(shape)


def per_device(
    feats, w_hidden, w_embed, items, teacher, block_counts, tail_rows, cand_owner, cand_block
):
    n_shard, n_sub = lax.axis_size("shard"), lax.axis_size("sub")
    q_dev = feats.shape[0]
    slots = cand_owner.shape[0]
    rows = n_shard * n_sub * CAP
    counts = block_counts[0]
    ends = jnp.cumsum(counts)
    pos = jnp.arange(slots, dtype=jnp.int32)[:, None]
    member = jnp.logical_and(pos < ends[None, :], pos >= (ends - counts)[None, :])
    used = jnp.where(pos == (ends - 1)[None, :], tail_rows[None, :], BLK)
    slot_used = jnp.sum(jnp.where(member, used, 0), axis=1, keepdims=True)
    valid = jnp.arange(BLK, dtype=jnp.int32)[None, :] < slot_used
    n_cand = ((counts - 1) * BLK + tail_rows).astype(F32)
    logit = teacher.astype(F32)
    top = jnp.max(jnp.where(valid, logit, -jnp.inf), axis=1, keepdims=True)
    query_top = jnp.max(jnp.where(member, top, -jnp.inf), axis=0, keepdims=True)
    slot_top = jnp.sum(jnp.where(member, query_top, 0.0), axis=1, keepdims=True)
    expo = jnp.where(valid, jnp.exp(logit - slot_top), 0.0)
    total = jnp.sum(
        jnp.where(member, jnp.sum(expo, axis=1, keepdims=True), 0.0), axis=0, keepdims=True
    )
    factor = jnp.sum(jnp.where(member, n_cand[None, :] / total, 0.0), axis=1, keepdims=True)
    teacher_n = expo * factor
    owner = cand_owner[:, 0]
    earlier = jnp.logical_and(owner[None, :] == owner[:, None], pos.T < pos)
    rank = jnp.sum(earlier.astype(jnp.int32), axis=1)
    dest = owner * CAP + rank
    place = jnp.arange(rows, dtype=jnp.int32)[:, None] == dest[None, :]
    info = jnp.sum(jnp.where(place, (cand_block * 256 + slot_used[:, 0])[None, :], 0), axis=1)
    member_row = nn(place.astype(BF16), member.astype(BF16))
    info_in = exchange(info)[:, None]
    teacher_in = exchange(nn(place.astype(F32), teacher_n, HI))
    block_in, used_in = info_in // 256, info_in % 256
    valid_in = jnp.arange(BLK, dtype=jnp.int32)[None, :] < used_in
    lane_block = jnp.arange(BLK_DEV * BLK, dtype=jnp.int32)[None, :] // BLK
    picked = lane_block == block_in

    def spread(values):
        return jnp.where(picked, jnp.tile(values, (1, BLK_DEV)), 0.0).astype(BF16)

    teacher_dq = exchange(nn(spread(teacher_in), items))
    query_teacher = tn(member_row, teacher_dq, HI)
    gathered = lax.all_gather(feats, "sub", axis=0, tiled=True)
    preact = nn(gathered, w_hidden)
    hidden = jax.nn.silu(preact).astype(BF16)
    emb_raw = lax.psum_scatter(nn(hidden, w_embed), "sub", scatter_dimension=0, tiled=True)
    inv_rms = lax.rsqrt(jnp.mean(emb_raw * emb_raw, axis=1, keepdims=True) + EPS)
    query_emb = (emb_raw * inv_rms).astype(BF16)
    query_in = exchange(nn(member_row.astype(BF16), query_emb).astype(BF16))
    every = nt(query_in, items)
    scores = jnp.zeros((rows, BLK), F32)
    for block in range(BLK_DEV):
        scores = jnp.where(block_in == block, every[:, block * BLK : (block + 1) * BLK], scores)
    row_top = jnp.max(jnp.where(valid_in, scores, -1e30), axis=1, keepdims=True)
    expo = jnp.where(valid_in, jnp.exp(scores - row_top), 0.0)
    row_total = jnp.maximum(jnp.sum(expo, axis=1, keepdims=True), 1e-30)
    row_lse = row_top + jnp.log(row_total)
    mean_item = nn(spread(expo / row_total), items)
    mean_in = exchange(mean_item)
    lse_in = exchange(row_lse)
    mine = member_row > 0.5
    query_max = jnp.max(jnp.where(mine, lse_in, -jnp.inf), axis=0, keepdims=True)
    row_max = jnp.sum(jnp.where(mine, query_max, 0.0), axis=1, keepdims=True)
    used_row = jnp.sum(member_row, axis=1, keepdims=True) > 0.5
    weight = jnp.where(used_row, jnp.exp(lse_in - row_max), 0.0)
    query_sum = jnp.sum(jnp.where(mine, weight, 0.0), axis=0, keepdims=True)
    scale = n_cand[None, :] / query_sum
    row_weight = jnp.where(mine, weight * scale, 0.0)
    query_gradient = tn(row_weight, mean_in, HI) - query_teacher
    shift = query_max - jnp.log(scale)
    row_shift = jnp.sum(jnp.where(mine, shift, 0.0), axis=1, keepdims=True)
    shift_in = exchange(row_shift)
    dlogit = jnp.where(valid_in, jnp.exp(scores - shift_in), 0.0) - teacher_in
    grad_items = tn(spread(dlogit), query_in)
    grad_emb = (
        inv_rms
        * (
            query_gradient
            - emb_raw
            * inv_rms
            * inv_rms
            * jnp.mean(query_gradient * emb_raw, axis=1, keepdims=True)
        )
    ).astype(BF16)
    grad_emb_all = lax.all_gather(grad_emb, "sub", axis=0, tiled=True)
    embed_term = tn(hidden, grad_emb_all)
    dhidden = nt(grad_emb_all, w_embed)
    sig = jax.nn.sigmoid(preact)
    grad_pre = (dhidden * sig * (1.0 + preact * (1.0 - sig))).astype(BF16)
    grad_feats = lax.psum_scatter(
        nt(grad_pre, w_hidden).astype(BF16), "sub", scatter_dimension=0, tiled=True
    ).astype(F32)
    hidden_term = tn(gathered, grad_pre).astype(BF16)
    width = hidden_term.shape[1]
    joined = jnp.concatenate(
        [
            hidden_term.reshape(n_shard, -1, width),
            embed_term.astype(BF16).reshape(n_shard, -1, width),
        ],
        axis=1,
    )
    joined = lax.psum_scatter(joined, "shard", scatter_dimension=0, tiled=False)
    depth = hidden_term.shape[0] // n_shard
    grad_hidden = joined[:depth].astype(F32)
    embed_part = joined[depth:].reshape(-1, embed_term.shape[1])
    grad_embed = lax.all_gather(embed_part, "shard", axis=0, tiled=True).astype(F32)
    return (grad_feats, grad_hidden, grad_embed, grad_items)


def solution(mesh):
    both = ("shard", "sub")
    placed = (
        P(both, None),
        P(None, "sub"),
        P("sub", None),
        P(both, None),
        P(both, None),
        P(both, None),
        P(both),
        P(both, None),
        P(both),
    )
    return jax.shard_map(
        per_device,
        mesh=mesh,
        in_specs=placed,
        out_specs=(P(both, None), P("shard", "sub"), P("sub", None), P(both, None)),
        check_vma=False,
    )
```

```python
import functools

import jax
import jax.numpy as jnp
from jax import lax
from jax.experimental import pallas as pl
from jax.experimental.pallas import tpu as pltpu
from jax.sharding import PartitionSpec as P

BLK = 128
BLK_DEV = 8
CAP = 2
EPS = 1e-06
F32 = jnp.float32
BF16 = jnp.bfloat16
I32 = jnp.int32
MESH = pl.DeviceIdType.MESH
STAGES = (
    "feats", "emb", "e1a", "e1b", "e2b", "e2a", "e3a", "e3b", "e4b", "e4a", "e5a", "e5b",
    "px", "fx", "gy", "gx", "core", "zs", "gf0", "gf1", "gf2", "gf3", "er", "eb", "ex",
)


def dot(left, right, left_dim, right_dim):
    return lax.dot_general(
        left, right, (((left_dim,), (right_dim,)), ((), ())), preferred_element_type=F32
    )


def nn(left, right):
    return dot(left, right, 1, 0)


def tn(left, right):
    return dot(left, right, 0, 0)


def nt(left, right):
    return dot(left, right, 1, 1)


def iota(shape, axis):
    return lax.broadcasted_iota(I32, shape, axis)


def pieces(value):
    high = value.astype(BF16).astype(F32)
    rest = value - high
    middle = rest.astype(BF16).astype(F32)
    return high, middle, rest - middle


def in_lanes(columns, rows):
    lane = iota((rows, 128), 1)
    result = jnp.zeros((rows, 128), F32)
    for place, column in enumerate(columns):
        result = jnp.where(lane == place, column, result)
    return result


def kernel(n_z, n_x, n_y, names, *refs):
    r = dict(zip(names, refs))
    feats, w_hbm, w_embed, items = r["feats"], r["w_hidden"], r["w_embed"], r["items"]
    n_a, n_b = n_x * n_y, n_z * 2
    rows = n_a * n_b * CAP
    q_dev, depth = feats.shape
    units = w_hbm.shape[1]
    emb = w_embed.shape[1]
    slots = r["teacher"].shape[0]
    block_cols = depth // (n_z * n_x)
    half = block_cols // 2

    shard, y = lax.axis_index("shard"), lax.axis_index("sub")
    core = lax.rem(shard, 2)
    x = lax.rem(shard // 2, n_x)
    z = shard // (2 * n_x)
    a = x * n_y + y
    b = z * 2 + core

    def at(z_, x_, core_, y_):
        return ((z_ * n_x + x_) * 2 + core_, y_)

    groups = {
        "y": (n_y, y, lambda p: at(z, x, core, p)),
        "x": (n_x, x, lambda p: at(z, p, core, y)),
        "z": (n_z, z, lambda p: at(p, x, core, y)),
        "a": (n_a, a, lambda p: at(z, p // n_y, core, lax.rem(p, n_y))),
        "b": (n_b, b, lambda p: at(p // 2, x, lax.rem(p, 2), y)),
    }
    send_sem, recv_sem = r["send_sem"], r["recv_sem"]
    pending = []

    def remote(stage, source, target, send_at, recv_at, device):
        row = STAGES.index(stage)
        return pltpu.make_async_remote_copy(
            src_ref=source,
            dst_ref=target,
            send_sem=send_sem.at[row, send_at],
            recv_sem=recv_sem.at[row, recv_at],
            device_id=device,
            device_id_type=MESH,
        )

    def each(group, body):
        size, me, device = groups[group]

        def step(j, carry):
            body(lax.rem(me + j, size), me, device)
            return carry

        lax.fori_loop(1, size, step, 0)

    def send(stage, group, source, target):
        def start(p, me, device):
            remote(stage, source(p), target(me), p, me, device(p)).start()

        each(group, start)

        def finish():
            def wait(p, me, device):
                remote(stage, source(p), target(me), p, me, device(p)).wait_send()

            each(group, wait)

        pending.append(finish)

    def receive(stage, group, target):
        def wait(p, me, device):
            remote(stage, target(p), target(p), p, p, device(p)).wait_recv()

        each(group, wait)

    weights = r["weights"]
    load = pltpu.make_async_copy(w_hbm, weights, r["load_sem"])
    load.start()
    barrier = pltpu.get_barrier_semaphore()
    for group in ("a", "b"):
        each(
            group,
            lambda p, me, device: pl.semaphore_signal(
                barrier, inc=1, device_id=device(p), device_id_type=MESH
            ),
        )
    feats_y = r["feats_y"]
    feats_y[y] = feats[...]
    pl.semaphore_wait(barrier, n_a + n_b - 2)
    send("feats", "y", lambda p: feats, lambda me: feats_y.at[me])

    perm = r["perm"]
    log_a, log_b = n_a.bit_length() - 1, n_b.bit_length() - 1
    line = iota((rows, rows), 0)
    from_row = (
        jnp.bitwise_and(line >> 1, n_a - 1) * (2 * n_b)
        + (line >> (1 + log_a)) * 2
        + jnp.bitwise_and(line, 1)
    )
    perm[...] = jnp.where(from_row == iota((rows, rows), 1), 1.0, 0.0).astype(BF16)

    def first(name, forward):
        group, size = ("a", n_a) if forward else ("b", n_b)
        source, target = r[name + "_s1"], r[name + "_r1"]
        me = groups[group][1]
        send(name + group, group, lambda p: source.at[p], lambda m: target.at[m])
        target[me] = source[me]

    def second(name, forward):
        group, size = ("a", n_a) if forward else ("b", n_b)
        other, other_size = ("b", n_b) if forward else ("a", n_a)
        middle = r[name + "_r1"]
        receive(name + group, group, lambda p: middle.at[p])
        source, target = r[name + "_s2"], r[name + "_r2"]
        lanes = middle.shape[2]
        moved = nn(perm[...], middle[...].reshape(rows, lanes)).astype(BF16)
        source[...] = moved.reshape(other_size, rows // other_size, lanes)
        me = groups[other][1]
        send(name + other, other, lambda p: source.at[p], lambda m: target.at[m])
        target[me] = source[me]

    def third(name, forward):
        other = "b" if forward else "a"
        target = r[name + "_r2"]
        receive(name + other, other, lambda p: target.at[p])
        return target

    counts = r["counts"][...].astype(F32)
    tails = r["tails"][...].astype(F32)
    triangle = jnp.where(iota((q_dev, q_dev), 0) <= iota((q_dev, q_dev), 1), 1.0, 0.0)
    ends = nn(jnp.broadcast_to(counts, (8, q_dev)).astype(BF16), triangle.astype(BF16))[0:1]
    starts = ends - counts
    pos = iota((slots, q_dev), 0).astype(F32)
    member = jnp.logical_and(pos < ends, pos >= starts)
    used = jnp.where(pos == ends - 1.0, tails, float(BLK))
    slot_used = jnp.sum(jnp.where(member, used, 0.0), axis=1, keepdims=True)
    valid = iota((slots, BLK), 1).astype(F32) < slot_used
    n_cand = (counts - 1.0) * BLK + tails
    logit = r["teacher"][...].astype(F32)
    top = jnp.max(jnp.where(valid, logit, -1e30), axis=1, keepdims=True)
    query_top = jnp.max(jnp.where(member, top, -1e30), axis=0, keepdims=True)
    slot_top = jnp.sum(jnp.where(member, query_top, 0.0), axis=1, keepdims=True)
    expo = jnp.where(valid, jnp.exp(logit - slot_top), 0.0)
    slot_sum = jnp.sum(expo, axis=1, keepdims=True)
    total = jnp.sum(jnp.where(member, slot_sum, 0.0), axis=0, keepdims=True)
    query_shift = query_top + jnp.log(total / n_cand)
    slot_shift = jnp.sum(jnp.where(member, query_shift, 0.0), axis=1, keepdims=True)
    owner = r["owner"][...]
    same = jnp.logical_and(
        r["owner_row"][...] == owner, iota((slots, slots), 1) < iota((slots, slots), 0)
    )
    rank = jnp.sum(jnp.where(same, 1.0, 0.0), axis=1, keepdims=True)
    log_y, log_x = n_y.bit_length() - 1, n_x.bit_length() - 1
    owner_y = jnp.bitwise_and(owner, n_y - 1)
    owner_core = jnp.bitwise_and(owner >> log_y, 1)
    owner_x = jnp.bitwise_and(owner >> (log_y + 1), n_x - 1)
    owner_z = owner >> (log_y + 1 + log_x)
    base = ((owner_x * n_y + owner_y) * n_b + owner_z * 2 + owner_core) * CAP
    dest = base.astype(F32) + rank
    place = jnp.where(dest == iota((slots, rows), 1).astype(F32), 1.0, 0.0).astype(BF16)
    side = in_lanes((r["block"][...].astype(F32), slot_used) + pieces(slot_shift), slots)
    payload = jnp.concatenate([logit, side], axis=1).astype(BF16)
    r["e1_s1"][...] = tn(place, payload).astype(BF16).reshape(r["e1_s1"].shape)
    first("e1", True)
    member_row = r["member_row"]
    member_row[...] = tn(place, jnp.where(member, 1.0, 0.0).astype(BF16))
    second("e1", True)

    receive("feats", "y", lambda p: feats_y.at[p])
    load.wait()
    preact, preact_x = r["preact"], r["preact_x"]
    group_rows = n_y * q_dev
    everyone = feats_y[...].reshape(group_rows, depth)
    step_units = min(256, units)

    def forward(j, total_emb):
        columns = pl.ds(pl.multiple_of(j * step_units, step_units), step_units)
        part = nn(everyone, weights[:, columns])
        preact[:, columns] = part
        hidden = (part / (1.0 + jnp.exp(-part))).astype(BF16)
        return total_emb + nn(hidden, w_embed[columns, :])

    emb_part = lax.fori_loop(
        0, units // step_units, forward, jnp.zeros((group_rows, emb), F32)
    )
    emb_s, emb_r = r["emb_s"], r["emb_r"]
    emb_s[...] = emb_part.reshape(n_y, q_dev, emb)
    send("emb", "y", lambda p: emb_s.at[p], lambda me: emb_r.at[me])
    emb_r[y] = emb_s[y]

    chunks = max(1, rows // 128)
    per = n_b // chunks
    chunk_rows = rows // chunks

    def lift(values, block_in):
        parts = [jnp.where(block_in == float(k), values, 0.0).astype(BF16) for k in range(BLK_DEV)]
        return jnp.concatenate(parts, axis=1)

    sent = third("e1", True)
    teacher_n, info, spread = r["teacher_n"], r["info"], r["spread"]

    def chunk_of(ref, j):
        return ref[pl.ds(j * per, per)].reshape(chunk_rows, ref.shape[2])

    def rows_of(j):
        return pl.ds(pl.multiple_of(j * chunk_rows, chunk_rows), chunk_rows)

    def teacher_part(j, carry):
        chunk = chunk_of(sent, j).astype(F32)
        notes = chunk[:, BLK : 2 * BLK]
        block_in, used_in = notes[:, 0:1], notes[:, 1:2]
        shift_in = notes[:, 2:3] + notes[:, 3:4] + notes[:, 4:5]
        valid_in = iota((chunk_rows, BLK), 1).astype(F32) < used_in
        probs = jnp.where(valid_in, jnp.exp(chunk[:, :BLK] - shift_in), 0.0)
        teacher_n[rows_of(j), :] = probs
        info[rows_of(j), :] = notes
        term = nn(lift(probs, block_in), items[...])
        r["e2_s1"][pl.ds(j * per, per)] = term.astype(BF16).reshape(per, 2 * n_a, emb)
        return carry

    lax.fori_loop(0, chunks, teacher_part, 0)
    first("e2", False)

    receive("emb", "y", lambda p: emb_r.at[p])
    emb_raw = jnp.sum(emb_r[...], axis=0)
    inv_rms = lax.rsqrt(jnp.mean(emb_raw * emb_raw, axis=1, keepdims=True) + EPS)
    query_emb = (emb_raw * inv_rms).astype(BF16)
    member_bf = member_row[...].astype(BF16)
    r["e3_s1"][...] = nn(member_bf, query_emb).astype(BF16).reshape(r["e3_s1"].shape)
    first("e3", True)
    second("e2", False)
    preact_x[x] = preact[...].astype(BF16)
    feats_s, feats_x = r["feats_s"], r["feats_x"]
    for p in range(n_x):
        for k in range(n_z):
            column = (k * n_x + p) * block_cols
            feats_s[p, :, k * block_cols : (k + 1) * block_cols] = feats_y[
                :, :, column : column + block_cols
            ].reshape(group_rows, block_cols)
    second("e3", True)
    send("px", "x", lambda p: preact_x.at[x], lambda me: preact_x.at[me])
    send("fx", "x", lambda p: feats_s.at[p], lambda me: feats_x.at[me])
    feats_x[x] = feats_s[x]
    back = third("e2", False)
    query_teacher = tn(member_bf, back[...].reshape(rows, emb))

    queries = third("e3", True)
    scores = r["scores"]

    def score_part(j, carry):
        every = nt(chunk_of(queries, j), items[...])
        notes = info[rows_of(j), :]
        block_in, used_in = notes[:, 0:1], notes[:, 1:2]
        picked = jnp.zeros((chunk_rows, BLK), F32)
        for k in range(BLK_DEV):
            picked = jnp.where(block_in == float(k), every[:, k * BLK : (k + 1) * BLK], picked)
        valid_in = iota((chunk_rows, BLK), 1).astype(F32) < used_in
        row_top = jnp.max(jnp.where(valid_in, picked, -1e30), axis=1, keepdims=True)
        row_expo = jnp.where(valid_in, jnp.exp(picked - row_top), 0.0)
        row_sum = jnp.maximum(jnp.sum(row_expo, axis=1, keepdims=True), 1e-30)
        scores[rows_of(j), :] = picked
        term = nn(lift(row_expo / row_sum, block_in), items[...])
        empty = used_in < 0.5
        lse = jnp.where(empty, 0.0, row_top + jnp.log(row_sum))
        message = jnp.concatenate([term, in_lanes(pieces(lse), chunk_rows)], axis=1)
        r["e4_s1"][pl.ds(j * per, per)] = message.astype(BF16).reshape(per, 2 * n_a, emb + 128)
        return carry

    lax.fori_loop(0, chunks, score_part, 0)
    first("e4", False)
    second("e4", False)
    returned = third("e4", False)[...].reshape(rows, emb + 128)

    lse_bits = returned[:, emb : emb + 128].astype(F32)
    lse_in = lse_bits[:, 0:1] + lse_bits[:, 1:2] + lse_bits[:, 2:3]
    mine = member_row[...] > 0.5
    query_max = jnp.max(jnp.where(mine, lse_in, -1e30), axis=0, keepdims=True)
    weight = jnp.where(mine, jnp.exp(lse_in - query_max), 0.0)
    scale = n_cand / jnp.sum(weight, axis=0, keepdims=True)
    weight = weight * scale
    weight_high = weight.astype(BF16)
    weight_low = (weight - weight_high.astype(F32)).astype(BF16)
    mean_item = returned[:, :emb]
    gradient = tn(weight_high, mean_item) + tn(weight_low, mean_item) - query_teacher
    grad_emb = (
        inv_rms
        * (
            gradient
            - emb_raw * inv_rms * inv_rms * jnp.mean(gradient * emb_raw, axis=1, keepdims=True)
        )
    ).astype(BF16)
    grad_y, grad_x = r["grad_y"], r["grad_x"]
    grad_y[y] = grad_emb
    send("gy", "y", lambda p: grad_y.at[y], lambda me: grad_y.at[me])
    shift = query_max - jnp.log(scale)
    row_shift = jnp.sum(jnp.where(mine, shift, 0.0), axis=1, keepdims=True)
    r["e5_s1"][...] = in_lanes(pieces(row_shift), rows).astype(BF16).reshape(r["e5_s1"].shape)
    first("e5", True)
    receive("gy", "y", lambda p: grad_y.at[p])
    grad_group = grad_y[...].reshape(group_rows, emb)
    grad_x[x] = grad_group
    send("gx", "x", lambda p: grad_x.at[x], lambda me: grad_x.at[me])

    def derivative(dhidden, before):
        sig = 1.0 / (1.0 + jnp.exp(-before))
        return (dhidden * sig * (1.0 + before * (1.0 - sig))).astype(BF16)

    grad_pre = derivative(nt(grad_group, w_embed[...]), preact[...])
    gf_s, gf_r = r["gf_s"], r["gf_r"]
    step_depth = min(256, depth // 4)

    def feats_part(part):
        quarter = depth // 4

        def step(j, carry):
            start = pl.multiple_of(part * quarter + j * step_depth, step_depth)
            value = nt(grad_pre, weights[pl.ds(start, step_depth), :])
            gf_s[:, :, pl.ds(start, step_depth)] = value.astype(BF16).reshape(
                n_y, q_dev, step_depth
            )
            return carry

        lax.fori_loop(0, quarter // step_depth, step, 0)
        columns = pl.ds(part * quarter, quarter)
        send(
            "gf" + str(part),
            "y",
            lambda p: gf_s.at[p, :, columns],
            lambda me: gf_r.at[me, :, columns],
        )

    feats_part(0)
    second("e5", True)
    receive("px", "x", lambda p: preact_x.at[p])
    receive("fx", "x", lambda p: feats_x.at[p])
    receive("gx", "x", lambda p: grad_x.at[p])

    pre_x = r["pre_x"]

    def pre_part(j, carry):
        pre_x[j] = derivative(nt(grad_x[j], w_embed[...]), preact_x[j].astype(F32))
        return carry

    lax.fori_loop(0, n_x, pre_part, 0)
    line_rows = n_x * group_rows
    halves, halves_bf, core_r = r["halves"], r["halves_bf"], r["core_r"]
    mate = at(z, x, 1 - core, y)

    def core_copy(k):
        return remote("core", halves_bf.at[k, 1 - core], core_r.at[k], k, k, mate)

    def hidden_part(j, carry):
        k = lax.rem(z + n_z // 2 + j, n_z)
        columns = pl.ds(pl.multiple_of(k * block_cols, block_cols), block_cols)
        left = feats_x[:, :, columns].reshape(line_rows, block_cols)
        value = tn(left, pre_x[...].reshape(line_rows, units)).reshape(2, half, units)
        halves[k] = value
        halves_bf[k] = value.astype(BF16)
        core_copy(k).start()
        return carry

    lax.fori_loop(0, n_z, hidden_part, 0)
    pending.append(
        lambda: lax.fori_loop(0, n_z, lambda k, s: (core_copy(k).wait_send(), s)[1], 0)
    )
    z_s, z_r = r["z_s"], r["z_r"]

    def z_copy(k):
        return remote("zs", z_s.at[k], z_r.at[z], k, z, at(k, x, core, y))

    def z_step(j, carry):
        k = lax.rem(z + n_z // 2 + j, n_z)
        core_copy(k).wait_recv()
        z_s[k] = (halves[k, core] + core_r[k].astype(F32)).astype(BF16)

        @pl.when(k != z)
        def _():
            z_copy(k).start()

        return carry

    lax.fori_loop(0, n_z, z_step, 0)
    pending.append(lambda: each("z", lambda p, me, device: z_copy(p).wait_send()))
    own = halves[z, core] + core_r[z].astype(F32)

    part_units = units // n_x
    mine_units = pl.ds(pl.multiple_of(x * part_units, part_units), part_units)
    before = preact_x[:, :, mine_units].astype(F32).reshape(line_rows, part_units)
    hidden_x = (before / (1.0 + jnp.exp(-before))).astype(BF16)
    er_s, er_r, eb, ex = r["er_s"], r["er_r"], r["eb"], r["ex"]
    er_s[...] = (
        tn(hidden_x, grad_x[...].reshape(line_rows, emb)).astype(BF16).reshape(er_s.shape)
    )
    send("er", "b", lambda p: er_s.at[p], lambda me: er_r.at[me])
    er_r[b] = er_s[b]
    feats_part(1)
    feats_part(2)
    receive("er", "b", lambda p: er_r.at[p])
    eb[b] = jnp.sum(er_r[...].astype(F32), axis=0).astype(BF16)
    send("eb", "b", lambda p: eb.at[b], lambda me: eb.at[me])
    feats_part(3)

    shifts = third("e5", True)

    def item_part(j, carry):
        notes = info[rows_of(j), :]
        block_in, used_in = notes[:, 0:1], notes[:, 1:2]
        bits = chunk_of(shifts, j).astype(F32)
        shift_in = bits[:, 0:1] + bits[:, 1:2] + bits[:, 2:3]
        valid_in = iota((chunk_rows, BLK), 1).astype(F32) < used_in
        student = jnp.where(valid_in, jnp.exp(scores[rows_of(j), :] - shift_in), 0.0)
        spread[rows_of(j), :] = lift(student - teacher_n[rows_of(j), :], block_in)
        return carry

    lax.fori_loop(0, chunks, item_part, 0)

    def item_block(j, carry):
        columns = pl.ds(pl.multiple_of(j * 256, 256), 256)
        r["grad_items"][columns, :] = tn(
            spread[:, columns], queries[...].reshape(rows, emb)
        )
        return carry

    lax.fori_loop(0, BLK_DEV * BLK // 256, item_block, 0)
    receive("eb", "b", lambda p: eb.at[p])
    ex[x] = eb[...].reshape(part_units, emb)
    send("ex", "x", lambda p: ex.at[x], lambda me: ex.at[me])
    for part in range(4):
        columns = pl.ds(part * (depth // 4), depth // 4)
        receive("gf" + str(part), "y", lambda p: gf_r.at[p, :, columns])
    gf_r[y] = gf_s[y]
    r["grad_feats"][...] = jnp.sum(gf_r[...].astype(F32), axis=0)
    receive("ex", "x", lambda p: ex.at[p])
    r["grad_embed"][...] = ex[...].astype(F32).reshape(units, emb)
    each(
        "z",
        lambda p, me, device: remote(
            "zs", z_r.at[p], z_r.at[p], p, p, device(p)
        ).wait_recv(),
    )
    z_r[z] = jnp.zeros((half, units), BF16)
    r["grad_hidden"][...] = own + jnp.sum(z_r[...].astype(F32), axis=0)
    for finish in pending:
        finish()


def per_device(
    n_z, n_x, n_y, feats, w_hidden, w_embed, items, teacher, block_counts, tail_rows,
    cand_owner, cand_block,
):
    q_dev, depth = feats.shape
    units, emb = w_embed.shape
    slots = cand_owner.shape[0]
    n_a, n_b = n_x * n_y, n_z * 2
    rows = n_a * n_b * CAP
    group_rows = n_y * q_dev
    block_cols = depth // (n_z * n_x)
    half = block_cols // 2
    part_units = units // n_x
    inputs = {
        "feats": feats,
        "w_hidden": w_hidden,
        "w_embed": w_embed,
        "items": items,
        "teacher": teacher,
        "counts": block_counts,
        "tails": tail_rows.reshape(1, q_dev),
        "owner": cand_owner,
        "owner_row": cand_owner.reshape(1, slots),
        "block": cand_block.reshape(slots, 1),
    }
    outputs = {
        "grad_feats": (q_dev, depth),
        "grad_hidden": (half, units),
        "grad_embed": (units, emb),
        "grad_items": (BLK_DEV * BLK, emb),
    }
    vmem = {
        "weights": ((depth, units), BF16),
        "feats_y": ((n_y, q_dev, depth), BF16),
        "perm": ((rows, rows), BF16),
        "member_row": ((rows, q_dev), F32),
        "preact": ((group_rows, units), F32),
        "preact_x": ((n_x, group_rows, units), BF16),
        "emb_s": ((n_y, q_dev, emb), F32),
        "emb_r": ((n_y, q_dev, emb), F32),
        "teacher_n": ((rows, BLK), F32),
        "info": ((rows, 128), F32),
        "spread": ((rows, BLK_DEV * BLK), BF16),
        "feats_s": ((n_x, group_rows, n_z * block_cols), BF16),
        "feats_x": ((n_x, group_rows, n_z * block_cols), BF16),
        "scores": ((rows, BLK), F32),
        "grad_y": ((n_y, q_dev, emb), BF16),
        "grad_x": ((n_x, group_rows, emb), BF16),
        "gf_s": ((n_y, q_dev, depth), BF16),
        "gf_r": ((n_y, q_dev, depth), BF16),
        "pre_x": ((n_x, group_rows, units), BF16),
        "halves": ((n_z, 2, half, units), F32),
        "halves_bf": ((n_z, 2, half, units), BF16),
        "core_r": ((n_z, half, units), BF16),
        "z_s": ((n_z, half, units), BF16),
        "z_r": ((n_z, half, units), BF16),
        "er_s": ((n_b, part_units // n_b, emb), BF16),
        "er_r": ((n_b, part_units // n_b, emb), BF16),
        "eb": ((n_b, part_units // n_b, emb), BF16),
        "ex": ((n_x, part_units, emb), BF16),
    }
    for name, lanes, ahead in (
        ("e1", 256, True),
        ("e2", emb, False),
        ("e3", emb, True),
        ("e4", emb + 128, False),
        ("e5", 128, True),
    ):
        one, two = ((n_a, 2 * n_b, lanes), (n_b, 2 * n_a, lanes))
        if not ahead:
            one, two = two, one
        for suffix, shape in (("_s1", one), ("_r1", one), ("_s2", two), ("_r2", two)):
            vmem[name + suffix] = (shape, BF16)
    scratch = [pltpu.VMEM(shape, kind) for shape, kind in vmem.values()]
    most = max(n_a, n_b)
    scratch += [
        pltpu.SemaphoreType.DMA((len(STAGES), most)),
        pltpu.SemaphoreType.DMA((len(STAGES), most)),
        pltpu.SemaphoreType.DMA,
    ]
    names = list(inputs) + list(outputs) + list(vmem) + ["send_sem", "recv_sem", "load_sem"]
    specs = [
        pl.BlockSpec(memory_space=pl.ANY if name == "w_hidden" else pltpu.VMEM)
        for name in inputs
    ]
    return pl.pallas_call(
        functools.partial(kernel, n_z, n_x, n_y, names),
        out_shape=[jax.ShapeDtypeStruct(shape, F32) for shape in outputs.values()],
        in_specs=specs,
        out_specs=[pl.BlockSpec(memory_space=pltpu.VMEM)] * len(outputs),
        scratch_shapes=scratch,
        compiler_params=pltpu.CompilerParams(
            collective_id=0, has_side_effects=True, vmem_limit_bytes=58 * 1024 * 1024
        ),
    )(*inputs.values())


def solution(mesh):
    n_y = mesh.shape["sub"]
    n_x = n_y
    n_z = mesh.shape["shard"] // (2 * n_x)
    both = ("shard", "sub")
    placed = (
        P(both, None),
        P(None, "sub"),
        P("sub", None),
        P(both, None),
        P(both, None),
        P(both, None),
        P(both),
        P(both, None),
        P(both),
    )
    return jax.shard_map(
        functools.partial(per_device, n_z, n_x, n_y),
        mesh=mesh,
        in_specs=placed,
        out_specs=(P(both, None), P("shard", "sub"), P("sub", None), P(both, None)),
        check_vma=False,
    )
```

```python
import functools

import jax
import jax.numpy as jnp
from jax import lax
from jax.experimental import pallas as pl
from jax.experimental.pallas import tpu as pltpu
from jax.sharding import PartitionSpec as P

BLK = 128
BLK_DEV = 8
CAP = 2
EPS = 1e-06
F32 = jnp.float32
BF16 = jnp.bfloat16
I32 = jnp.int32
MESH = pl.DeviceIdType.MESH
STAGES = (
    "feats", "emb", "e1a", "e1b", "e2b", "e2a", "e3a", "e3b", "e4b", "e4a", "e5a", "e5b",
    "px", "fx", "ga", "core", "zs", "gf0", "gf1", "gf2", "gf3", "er", "eb", "ex",
)


def dot(left, right, left_dim, right_dim):
    return lax.dot_general(
        left, right, (((left_dim,), (right_dim,)), ((), ())), preferred_element_type=F32
    )


def nn(left, right):
    return dot(left, right, 1, 0)


def tn(left, right):
    return dot(left, right, 0, 0)


def nt(left, right):
    return dot(left, right, 1, 1)


def iota(shape, axis):
    return lax.broadcasted_iota(I32, shape, axis)


def pieces(value):
    high = value.astype(BF16).astype(F32)
    rest = value - high
    middle = rest.astype(BF16).astype(F32)
    return high, middle, rest - middle


def in_lanes(columns, rows):
    lane = iota((rows, 128), 1)
    result = jnp.zeros((rows, 128), F32)
    for place, column in enumerate(columns):
        result = jnp.where(lane == place, column, result)
    return result


def kernel(n_z, n_x, n_y, names, *refs):
    r = dict(zip(names, refs))
    feats, w_hbm, w_embed, items = r["feats"], r["w_hidden"], r["w_embed"], r["items"]
    n_a, n_b = n_x * n_y, n_z * 2
    rows = n_a * n_b * CAP
    q_dev, depth = feats.shape
    units = w_hbm.shape[1]
    emb = w_embed.shape[1]
    slots = r["teacher"].shape[0]
    block_cols = depth // (n_z * n_x)
    half = block_cols // 2

    shard, y = lax.axis_index("shard"), lax.axis_index("sub")
    core = lax.rem(shard, 2)
    x = lax.rem(shard // 2, n_x)
    z = shard // (2 * n_x)
    a = x * n_y + y
    b = z * 2 + core

    def at(z_, x_, core_, y_):
        return ((z_ * n_x + x_) * 2 + core_, y_)

    groups = {
        "y": (n_y, y, lambda p: at(z, x, core, p)),
        "x": (n_x, x, lambda p: at(z, p, core, y)),
        "z": (n_z, z, lambda p: at(p, x, core, y)),
        "a": (n_a, a, lambda p: at(z, p // n_y, core, lax.rem(p, n_y))),
        "b": (n_b, b, lambda p: at(p // 2, x, lax.rem(p, 2), y)),
    }
    send_sem, recv_sem = r["send_sem"], r["recv_sem"]
    pending = []

    def remote(stage, source, target, send_at, recv_at, device):
        row = STAGES.index(stage)
        return pltpu.make_async_remote_copy(
            src_ref=source,
            dst_ref=target,
            send_sem=send_sem.at[row, send_at],
            recv_sem=recv_sem.at[row, recv_at],
            device_id=device,
            device_id_type=MESH,
        )

    def each(group, body):
        size, me, device = groups[group]

        def step(j, carry):
            body(lax.rem(me + j, size), me, device)
            return carry

        lax.fori_loop(1, size, step, 0)

    def send(stage, group, source, target):
        def start(p, me, device):
            remote(stage, source(p), target(me), p, me, device(p)).start()

        each(group, start)

        def finish():
            def wait(p, me, device):
                remote(stage, source(p), target(me), p, me, device(p)).wait_send()

            each(group, wait)

        pending.append(finish)

    def receive(stage, group, target):
        def wait(p, me, device):
            remote(stage, target(p), target(p), p, p, device(p)).wait_recv()

        each(group, wait)

    weights = r["weights"]
    load = pltpu.make_async_copy(w_hbm, weights, r["load_sem"])
    load.start()
    barrier = pltpu.get_barrier_semaphore()
    for group in ("a", "b"):
        each(
            group,
            lambda p, me, device: pl.semaphore_signal(
                barrier, inc=1, device_id=device(p), device_id_type=MESH
            ),
        )
    feats_y = r["feats_y"]
    feats_y[y] = feats[...]

    perm = r["perm"]
    log_a, log_b = n_a.bit_length() - 1, n_b.bit_length() - 1
    line = iota((rows, rows), 0)
    from_row = (
        jnp.bitwise_and(line >> 1, n_a - 1) * (2 * n_b)
        + (line >> (1 + log_a)) * 2
        + jnp.bitwise_and(line, 1)
    )
    perm[...] = jnp.where(from_row == iota((rows, rows), 1), 1.0, 0.0).astype(BF16)

    def first(name, forward):
        group, size = ("a", n_a) if forward else ("b", n_b)
        source, target = r[name + "_s1"], r[name + "_r1"]
        me = groups[group][1]
        send(name + group, group, lambda p: source.at[p], lambda m: target.at[m])
        target[me] = source[me]

    def second(name, forward):
        group, size = ("a", n_a) if forward else ("b", n_b)
        other, other_size = ("b", n_b) if forward else ("a", n_a)
        middle = r[name + "_r1"]
        receive(name + group, group, lambda p: middle.at[p])
        source, target = r[name + "_s2"], r[name + "_r2"]
        lanes = middle.shape[2]
        moved = nn(perm[...], middle[...].reshape(rows, lanes)).astype(BF16)
        source[...] = moved.reshape(other_size, rows // other_size, lanes)
        me = groups[other][1]
        send(name + other, other, lambda p: source.at[p], lambda m: target.at[m])
        target[me] = source[me]

    def third(name, forward):
        other = "b" if forward else "a"
        target = r[name + "_r2"]
        receive(name + other, other, lambda p: target.at[p])
        return target

    counts = r["counts"][...].astype(F32)
    tails = r["tails"][...].astype(F32)
    triangle = jnp.where(iota((q_dev, q_dev), 0) <= iota((q_dev, q_dev), 1), 1.0, 0.0)
    ends = nn(jnp.broadcast_to(counts, (8, q_dev)).astype(BF16), triangle.astype(BF16))[0:1]
    starts = ends - counts
    pos = iota((slots, q_dev), 0).astype(F32)
    member = jnp.logical_and(pos < ends, pos >= starts)
    used = jnp.where(pos == ends - 1.0, tails, float(BLK))
    slot_used = jnp.sum(jnp.where(member, used, 0.0), axis=1, keepdims=True)
    valid = iota((slots, BLK), 1).astype(F32) < slot_used
    n_cand = (counts - 1.0) * BLK + tails
    logit = r["teacher"][...].astype(F32)
    top = jnp.max(jnp.where(valid, logit, -1e30), axis=1, keepdims=True)
    query_top = jnp.max(jnp.where(member, top, -1e30), axis=0, keepdims=True)
    slot_top = jnp.sum(jnp.where(member, query_top, 0.0), axis=1, keepdims=True)
    expo = jnp.where(valid, jnp.exp(logit - slot_top), 0.0)
    slot_sum = jnp.sum(expo, axis=1, keepdims=True)
    total = jnp.sum(jnp.where(member, slot_sum, 0.0), axis=0, keepdims=True)
    query_shift = query_top + jnp.log(total / n_cand)
    slot_shift = jnp.sum(jnp.where(member, query_shift, 0.0), axis=1, keepdims=True)
    diagonal = iota((slots, slots), 0) == iota((slots, slots), 1)
    owner_row = r["owner"][...]
    owner = jnp.sum(
        jnp.where(diagonal, owner_row.astype(F32), 0.0), axis=1, keepdims=True
    ).astype(I32)
    block = jnp.sum(
        jnp.where(diagonal, r["block"][...].astype(F32), 0.0), axis=1, keepdims=True
    )
    same = jnp.logical_and(
        owner_row == owner, iota((slots, slots), 1) < iota((slots, slots), 0)
    )
    rank = jnp.sum(jnp.where(same, 1.0, 0.0), axis=1, keepdims=True)
    log_y, log_x = n_y.bit_length() - 1, n_x.bit_length() - 1
    owner_y = jnp.bitwise_and(owner, n_y - 1)
    owner_core = jnp.bitwise_and(owner >> log_y, 1)
    owner_x = jnp.bitwise_and(owner >> (log_y + 1), n_x - 1)
    owner_z = owner >> (log_y + 1 + log_x)
    base = ((owner_x * n_y + owner_y) * n_b + owner_z * 2 + owner_core) * CAP
    dest = base.astype(F32) + rank
    place = jnp.where(dest == iota((slots, rows), 1).astype(F32), 1.0, 0.0).astype(BF16)
    side = in_lanes((block, slot_used) + pieces(slot_shift), slots)
    payload = jnp.concatenate([logit, side], axis=1).astype(BF16)
    placed = tn(place, payload).astype(BF16)
    r["e1_s1"][...] = nn(perm[...], placed).astype(BF16).reshape(r["e1_s1"].shape)
    member_row = r["member_row"]
    member_row[...] = tn(place, jnp.where(member, 1.0, 0.0).astype(BF16))
    pl.semaphore_wait(barrier, n_a + n_b - 2)
    send("feats", "y", lambda p: feats, lambda me: feats_y.at[me])
    first("e1", False)
    second("e1", False)

    receive("feats", "y", lambda p: feats_y.at[p])
    load.wait()
    preact, preact_x = r["preact"], r["preact_x"]
    group_rows = n_y * q_dev
    everyone = feats_y[...].reshape(group_rows, depth)
    step_units = min(256, units)

    def forward(j, total_emb):
        columns = pl.ds(pl.multiple_of(j * step_units, step_units), step_units)
        part = nn(everyone, weights[:, columns])
        preact[:, columns] = part
        hidden = (part / (1.0 + jnp.exp(-part))).astype(BF16)
        return total_emb + nn(hidden, w_embed[columns, :])

    emb_part = lax.fori_loop(
        0, units // step_units, forward, jnp.zeros((group_rows, emb), F32)
    )
    emb_s, emb_r = r["emb_s"], r["emb_r"]
    emb_s[...] = emb_part.reshape(n_y, q_dev, emb)
    send("emb", "y", lambda p: emb_s.at[p], lambda me: emb_r.at[me])
    emb_r[y] = emb_s[y]

    chunks = max(1, rows // 128)
    per = n_b // chunks
    chunk_rows = rows // chunks

    def lift(values, block_in):
        parts = [jnp.where(block_in == float(k), values, 0.0).astype(BF16) for k in range(BLK_DEV)]
        return jnp.concatenate(parts, axis=1)

    sent = r["e1_q"]
    by_owner = third("e1", False)[...].reshape(rows, 2 * BLK)
    sent[...] = nn(perm[...], by_owner).astype(BF16).reshape(sent.shape)
    teacher_n, info, spread = r["teacher_n"], r["info"], r["spread"]

    def chunk_of(ref, j):
        return ref[pl.ds(j * per, per)].reshape(chunk_rows, ref.shape[2])

    def rows_of(j):
        return pl.ds(pl.multiple_of(j * chunk_rows, chunk_rows), chunk_rows)

    def teacher_part(j, carry):
        chunk = chunk_of(sent, j).astype(F32)
        notes = chunk[:, BLK : 2 * BLK]
        block_in, used_in = notes[:, 0:1], notes[:, 1:2]
        shift_in = notes[:, 2:3] + notes[:, 3:4] + notes[:, 4:5]
        valid_in = iota((chunk_rows, BLK), 1).astype(F32) < used_in
        probs = jnp.where(valid_in, jnp.exp(chunk[:, :BLK] - shift_in), 0.0)
        teacher_n[rows_of(j), :] = probs
        info[rows_of(j), :] = notes
        term = nn(lift(probs, block_in), items[...])
        r["e2_s1"][pl.ds(j * per, per)] = term.astype(BF16).reshape(per, 2 * n_a, emb)
        return carry

    lax.fori_loop(0, chunks, teacher_part, 0)
    first("e2", False)

    receive("emb", "y", lambda p: emb_r.at[p])
    emb_raw = jnp.sum(emb_r[...], axis=0)
    inv_rms = lax.rsqrt(jnp.mean(emb_raw * emb_raw, axis=1, keepdims=True) + EPS)
    query_emb = (emb_raw * inv_rms).astype(BF16)
    member_bf = member_row[...].astype(BF16)
    r["e3_s1"][...] = nn(member_bf, query_emb).astype(BF16).reshape(r["e3_s1"].shape)
    first("e3", True)

    second("e2", False)
    second("e3", True)
    preact_x[x] = preact[...].astype(BF16)
    feats_s, feats_x = r["feats_s"], r["feats_x"]
    for p in range(n_x):
        for k in range(n_z):
            column = (k * n_x + p) * block_cols
            feats_s[p, :, k * block_cols : (k + 1) * block_cols] = feats_y[
                :, :, column : column + block_cols
            ].reshape(group_rows, block_cols)
    send("px", "x", lambda p: preact_x.at[x], lambda me: preact_x.at[me])
    send("fx", "x", lambda p: feats_s.at[p], lambda me: feats_x.at[me])
    feats_x[x] = feats_s[x]

    queries = third("e3", True)
    scores = r["scores"]

    def score_part(j, carry):
        every = nt(chunk_of(queries, j), items[...])
        notes = info[rows_of(j), :]
        block_in, used_in = notes[:, 0:1], notes[:, 1:2]
        picked = jnp.zeros((chunk_rows, BLK), F32)
        for k in range(BLK_DEV):
            picked = jnp.where(block_in == float(k), every[:, k * BLK : (k + 1) * BLK], picked)
        valid_in = iota((chunk_rows, BLK), 1).astype(F32) < used_in
        row_top = jnp.max(jnp.where(valid_in, picked, -1e30), axis=1, keepdims=True)
        row_expo = jnp.where(valid_in, jnp.exp(picked - row_top), 0.0)
        row_sum = jnp.maximum(jnp.sum(row_expo, axis=1, keepdims=True), 1e-30)
        scores[rows_of(j), :] = picked
        term = nn(lift(row_expo / row_sum, block_in), items[...])
        empty = used_in < 0.5
        lse = jnp.where(empty, 0.0, row_top + jnp.log(row_sum))
        message = jnp.concatenate([term, in_lanes(pieces(lse), chunk_rows)], axis=1)
        r["e4_s1"][pl.ds(j * per, per)] = message.astype(BF16).reshape(per, 2 * n_a, emb + 128)
        return carry

    lax.fori_loop(0, chunks, score_part, 0)
    first("e4", False)
    second("e4", False)
    back = third("e2", False)
    query_teacher = tn(member_bf, back[...].reshape(rows, emb))
    returned = third("e4", False)[...].reshape(rows, emb + 128)

    lse_bits = returned[:, emb : emb + 128].astype(F32)
    lse_in = lse_bits[:, 0:1] + lse_bits[:, 1:2] + lse_bits[:, 2:3]
    mine = member_row[...] > 0.5
    query_max = jnp.max(jnp.where(mine, lse_in, -1e30), axis=0, keepdims=True)
    weight = jnp.where(mine, jnp.exp(lse_in - query_max), 0.0)
    scale = n_cand / jnp.sum(weight, axis=0, keepdims=True)
    weight = weight * scale
    weight_high = weight.astype(BF16)
    weight_low = (weight - weight_high.astype(F32)).astype(BF16)
    mean_item = returned[:, :emb]
    gradient = tn(weight_high, mean_item) + tn(weight_low, mean_item) - query_teacher
    grad_emb = (
        inv_rms
        * (
            gradient
            - emb_raw * inv_rms * inv_rms * jnp.mean(gradient * emb_raw, axis=1, keepdims=True)
        )
    ).astype(BF16)
    grad_a = r["grad_a"]
    grad_a[a] = grad_emb
    send("ga", "a", lambda p: grad_a.at[a], lambda me: grad_a.at[me])
    shift = query_max - jnp.log(scale)
    row_shift = jnp.sum(jnp.where(mine, shift, 0.0), axis=1, keepdims=True)
    r["e5_s1"][...] = in_lanes(pieces(row_shift), rows).astype(BF16).reshape(r["e5_s1"].shape)
    first("e5", True)
    def derivative(dhidden, before):
        sig = 1.0 / (1.0 + jnp.exp(-before))
        return (dhidden * sig * (1.0 + before * (1.0 - sig))).astype(BF16)

    receive("px", "x", lambda p: preact_x.at[p])
    receive("fx", "x", lambda p: feats_x.at[p])
    receive("ga", "a", lambda p: grad_a.at[p])
    second("e5", True)
    grad_group = grad_a[pl.ds(x * n_y, n_y)].reshape(group_rows, emb)

    pre_x = r["pre_x"]

    def pre_part(j, carry):
        part = grad_a[pl.ds(j * n_y, n_y)].reshape(group_rows, emb)
        pre_x[j] = derivative(nt(part, w_embed[...]), preact_x[j].astype(F32))
        return carry

    lax.fori_loop(0, n_x, pre_part, 0)
    line_rows = n_x * group_rows

    part_units = units // n_x
    mine_units = pl.ds(pl.multiple_of(x * part_units, part_units), part_units)
    before = preact_x[:, :, mine_units].astype(F32).reshape(line_rows, part_units)
    hidden_x = (before / (1.0 + jnp.exp(-before))).astype(BF16)
    er_s, er_r, eb, ex = r["er_s"], r["er_r"], r["eb"], r["ex"]
    er_s[...] = tn(hidden_x, grad_a[...].reshape(line_rows, emb)).astype(BF16).reshape(er_s.shape)
    send("er", "b", lambda p: er_s.at[p], lambda me: er_r.at[me])
    er_r[b] = er_s[b]

    halves, halves_bf, core_r = r["halves"], r["halves_bf"], r["core_r"]
    z_s, z_r = r["z_s"], r["z_r"]
    mate = at(z, x, 1 - core, y)

    def core_copy(k):
        return remote("core", halves_bf.at[k, 1 - core], core_r.at[k], k, k, mate)

    def z_copy(k):
        return remote("zs", z_s.at[k], z_r.at[z], k, z, at(k, x, core, y))

    def block_at(j):
        return lax.rem(z + n_z // 2 + j, n_z)

    def hidden_part(j):
        k = block_at(j)
        columns = pl.ds(pl.multiple_of(k * block_cols, block_cols), block_cols)
        left = feats_x[:, :, columns].reshape(line_rows, block_cols)
        value = tn(left, pre_x[...].reshape(line_rows, units)).reshape(2, half, units)
        halves[k] = value
        halves_bf[k] = value.astype(BF16)
        core_copy(k).start()

    def z_part(j):
        k = block_at(j)
        core_copy(k).wait_recv()
        z_s[k] = (halves[k, core] + core_r[k].astype(F32)).astype(BF16)

        @pl.when(k != z)
        def _():
            z_copy(k).start()

    lead = n_z // 2
    for j in range(lead):
        hidden_part(j)
    receive("er", "b", lambda p: er_r.at[p])
    eb[b] = jnp.sum(er_r[...].astype(F32), axis=0).astype(BF16)
    send("eb", "b", lambda p: eb.at[b], lambda me: eb.at[me])

    def both_parts(j, carry):
        z_part(j)
        hidden_part(j + lead)
        return carry

    lax.fori_loop(0, n_z - lead, both_parts, 0)
    lax.fori_loop(n_z - lead, n_z, lambda j, carry: (z_part(j), carry)[1], 0)
    pending.append(
        lambda: lax.fori_loop(0, n_z, lambda k, s: (core_copy(k).wait_send(), s)[1], 0)
    )
    pending.append(lambda: each("z", lambda p, me, device: z_copy(p).wait_send()))
    own = halves[z, core] + core_r[z].astype(F32)

    grad_pre = derivative(nt(grad_group, w_embed[...]), preact[...])
    gf_s, gf_r = r["gf_s"], r["gf_r"]
    step_depth = min(256, depth // 4)

    def feats_part(part):
        quarter = depth // 4

        def step(j, carry):
            start = pl.multiple_of(part * quarter + j * step_depth, step_depth)
            value = nt(grad_pre, weights[pl.ds(start, step_depth), :])
            gf_s[:, :, pl.ds(start, step_depth)] = value.astype(BF16).reshape(
                n_y, q_dev, step_depth
            )
            return carry

        lax.fori_loop(0, quarter // step_depth, step, 0)
        columns = pl.ds(part * quarter, quarter)
        send(
            "gf" + str(part),
            "y",
            lambda p: gf_s.at[p, :, columns],
            lambda me: gf_r.at[me, :, columns],
        )
    for part in range(4):
        feats_part(part)
    receive("eb", "b", lambda p: eb.at[p])
    ex[x] = eb[...].reshape(part_units, emb)
    send("ex", "x", lambda p: ex.at[x], lambda me: ex.at[me])

    shifts = third("e5", True)

    def item_part(j, carry):
        notes = info[rows_of(j), :]
        block_in, used_in = notes[:, 0:1], notes[:, 1:2]
        bits = chunk_of(shifts, j).astype(F32)
        shift_in = bits[:, 0:1] + bits[:, 1:2] + bits[:, 2:3]
        valid_in = iota((chunk_rows, BLK), 1).astype(F32) < used_in
        student = jnp.where(valid_in, jnp.exp(scores[rows_of(j), :] - shift_in), 0.0)
        spread[rows_of(j), :] = lift(student - teacher_n[rows_of(j), :], block_in)
        return carry

    lax.fori_loop(0, chunks, item_part, 0)

    def item_block(j, carry):
        columns = pl.ds(pl.multiple_of(j * 256, 256), 256)
        r["grad_items"][columns, :] = tn(
            spread[:, columns], queries[...].reshape(rows, emb)
        )
        return carry

    lax.fori_loop(0, BLK_DEV * BLK // 256, item_block, 0)
    for part in range(4):
        columns = pl.ds(part * (depth // 4), depth // 4)
        receive("gf" + str(part), "y", lambda p: gf_r.at[p, :, columns])
    gf_r[y] = gf_s[y]
    r["grad_feats"][...] = jnp.sum(gf_r[...].astype(F32), axis=0)
    receive("ex", "x", lambda p: ex.at[p])
    r["grad_embed"][...] = ex[...].astype(F32).reshape(units, emb)
    each(
        "z",
        lambda p, me, device: remote(
            "zs", z_r.at[p], z_r.at[p], p, p, device(p)
        ).wait_recv(),
    )
    z_r[z] = jnp.zeros((half, units), BF16)
    r["grad_hidden"][...] = own + jnp.sum(z_r[...].astype(F32), axis=0)
    for finish in pending:
        finish()


def hand_on(*refs):
    count = len(refs) // 2
    for k in range(count):
        refs[count + k][...] = refs[k][...]


def per_device(
    n_z, n_x, n_y, feats, w_hidden, w_embed, items, teacher, block_counts, tail_rows,
    cand_owner, cand_block,
):
    q_dev, depth = feats.shape
    units, emb = w_embed.shape
    slots = cand_owner.shape[0]
    n_a, n_b = n_x * n_y, n_z * 2
    rows = n_a * n_b * CAP
    group_rows = n_y * q_dev
    block_cols = depth // (n_z * n_x)
    half = block_cols // 2
    part_units = units // n_x
    inputs = {
        "feats": feats,
        "w_hidden": w_hidden,
        "w_embed": w_embed,
        "items": items,
        "teacher": teacher,
        "counts": block_counts,
        "tails": tail_rows.reshape(1, q_dev),
        "owner": cand_owner.reshape(1, slots),
        "block": cand_block.reshape(1, slots),
    }
    outputs = {
        "grad_feats": (q_dev, depth),
        "grad_hidden": (half, units),
        "grad_embed": (units, emb),
        "grad_items": (BLK_DEV * BLK, emb),
    }
    vmem = {
        "weights": ((depth, units), BF16),
        "feats_y": ((n_y, q_dev, depth), BF16),
        "perm": ((rows, rows), BF16),
        "member_row": ((rows, q_dev), F32),
        "preact": ((group_rows, units), F32),
        "preact_x": ((n_x, group_rows, units), BF16),
        "emb_s": ((n_y, q_dev, emb), F32),
        "emb_r": ((n_y, q_dev, emb), F32),
        "teacher_n": ((rows, BLK), F32),
        "info": ((rows, 128), F32),
        "spread": ((rows, BLK_DEV * BLK), BF16),
        "feats_s": ((n_x, group_rows, n_z * block_cols), BF16),
        "feats_x": ((n_x, group_rows, n_z * block_cols), BF16),
        "scores": ((rows, BLK), F32),
        "e1_q": ((n_b, 2 * n_a, 2 * BLK), BF16),
        "grad_a": ((n_a, q_dev, emb), BF16),
        "gf_s": ((n_y, q_dev, depth), BF16),
        "gf_r": ((n_y, q_dev, depth), BF16),
        "pre_x": ((n_x, group_rows, units), BF16),
        "halves": ((n_z, 2, half, units), F32),
        "halves_bf": ((n_z, 2, half, units), BF16),
        "core_r": ((n_z, half, units), BF16),
        "z_s": ((n_z, half, units), BF16),
        "z_r": ((n_z, half, units), BF16),
        "er_s": ((n_b, part_units // n_b, emb), BF16),
        "er_r": ((n_b, part_units // n_b, emb), BF16),
        "eb": ((n_b, part_units // n_b, emb), BF16),
        "ex": ((n_x, part_units, emb), BF16),
    }
    for name, lanes, ahead in (
        ("e1", 256, False),
        ("e2", emb, False),
        ("e3", emb, True),
        ("e4", emb + 128, False),
        ("e5", 128, True),
    ):
        one, two = ((n_a, 2 * n_b, lanes), (n_b, 2 * n_a, lanes))
        if not ahead:
            one, two = two, one
        for suffix, shape in (("_s1", one), ("_r1", one), ("_s2", two), ("_r2", two)):
            vmem[name + suffix] = (shape, BF16)
    scratch = [pltpu.VMEM(shape, kind) for shape, kind in vmem.values()]
    most = max(n_a, n_b)
    scratch += [
        pltpu.SemaphoreType.DMA((len(STAGES), most)),
        pltpu.SemaphoreType.DMA((len(STAGES), most)),
        pltpu.SemaphoreType.DMA,
    ]
    names = list(inputs) + list(outputs) + list(vmem) + ["send_sem", "recv_sem", "load_sem"]
    specs = [
        pl.BlockSpec(memory_space=pl.ANY if name == "w_hidden" else pltpu.VMEM)
        for name in inputs
    ]
    results = pl.pallas_call(
        functools.partial(kernel, n_z, n_x, n_y, names),
        out_shape=[jax.ShapeDtypeStruct(shape, F32) for shape in outputs.values()],
        in_specs=specs,
        out_specs=[pl.BlockSpec(memory_space=pltpu.VMEM)] * len(outputs),
        scratch_shapes=scratch,
        compiler_params=pltpu.CompilerParams(
            collective_id=0, has_side_effects=True, vmem_limit_bytes=58 * 1024 * 1024
        ),
    )(*inputs.values())
    return pl.pallas_call(
        hand_on,
        out_shape=[jax.ShapeDtypeStruct(shape, F32) for shape in outputs.values()],
        in_specs=[pl.BlockSpec(memory_space=pltpu.VMEM)] * len(outputs),
        out_specs=[pl.BlockSpec(memory_space=pltpu.VMEM)] * len(outputs),
    )(*results)


def solution(mesh):
    n_y = mesh.shape["sub"]
    n_x = n_y
    n_z = mesh.shape["shard"] // (2 * n_x)
    both = ("shard", "sub")
    placed = (
        P(both, None),
        P(None, "sub"),
        P("sub", None),
        P(both, None),
        P(both, None),
        P(both, None),
        P(both),
        P(both, None),
        P(both),
    )
    return jax.shard_map(
        functools.partial(per_device, n_z, n_x, n_y),
        mesh=mesh,
        in_specs=placed,
        out_specs=(P(both, None), P("shard", "sub"), P("sub", None), P(both, None)),
        check_vma=False,
    )
```

```python
import functools

import jax
import jax.numpy as jnp
from jax import lax
from jax.experimental import pallas as pl
from jax.experimental.pallas import tpu as pltpu
from jax.sharding import PartitionSpec as P

BLK = 128
BLK_DEV = 8
CAP = 2
EPS = 1e-06
F32 = jnp.float32
BF16 = jnp.bfloat16
I32 = jnp.int32
MESH = pl.DeviceIdType.MESH
STAGES = (
    "feats", "emb", "e1a", "e1b", "e2b", "e2a", "e3a", "e3b", "e4b", "e4a", "e5a", "e5b",
    "px", "fx", "ga", "core", "zs", "gf0", "gf1", "gf2", "gf3", "er", "eb", "ex",
)


def dot(left, right, left_dim, right_dim):
    return lax.dot_general(
        left, right, (((left_dim,), (right_dim,)), ((), ())), preferred_element_type=F32
    )


def nn(left, right):
    return dot(left, right, 1, 0)


def tn(left, right):
    return dot(left, right, 0, 0)


def nt(left, right):
    return dot(left, right, 1, 1)


def iota(shape, axis):
    return lax.broadcasted_iota(I32, shape, axis)


def pieces(value):
    high = value.astype(BF16).astype(F32)
    rest = value - high
    middle = rest.astype(BF16).astype(F32)
    return high, middle, rest - middle


def in_lanes(columns, rows):
    lane = iota((rows, 128), 1)
    result = jnp.zeros((rows, 128), F32)
    for place, column in enumerate(columns):
        result = jnp.where(lane == place, column, result)
    return result


def kernel(n_z, n_x, n_y, names, *refs):
    r = dict(zip(names, refs))
    feats, w_hbm, w_embed, items = r["feats"], r["w_hidden"], r["w_embed"], r["items"]
    n_a, n_b = n_x * n_y, n_z * 2
    rows = n_a * n_b * CAP
    q_dev, depth = feats.shape
    units = w_hbm.shape[1]
    emb = w_embed.shape[1]
    slots = r["teacher"].shape[0]
    block_cols = depth // (n_z * n_x)
    half = block_cols // 2

    shard, y = lax.axis_index("shard"), lax.axis_index("sub")
    core = lax.rem(shard, 2)
    x = lax.rem(shard // 2, n_x)
    z = shard // (2 * n_x)
    a = x * n_y + y
    b = z * 2 + core

    def at(z_, x_, core_, y_):
        return ((z_ * n_x + x_) * 2 + core_, y_)

    groups = {
        "y": (n_y, y, lambda p: at(z, x, core, p)),
        "x": (n_x, x, lambda p: at(z, p, core, y)),
        "z": (n_z, z, lambda p: at(p, x, core, y)),
        "a": (n_a, a, lambda p: at(z, p // n_y, core, lax.rem(p, n_y))),
        "b": (n_b, b, lambda p: at(p // 2, x, lax.rem(p, 2), y)),
    }
    send_sem, recv_sem = r["send_sem"], r["recv_sem"]
    pending = []

    def remote(stage, source, target, send_at, recv_at, device):
        row = STAGES.index(stage)
        return pltpu.make_async_remote_copy(
            src_ref=source,
            dst_ref=target,
            send_sem=send_sem.at[row, send_at],
            recv_sem=recv_sem.at[row, recv_at],
            device_id=device,
            device_id_type=MESH,
        )

    def each(group, body):
        size, me, device = groups[group]

        def step(j, carry):
            body(lax.rem(me + j, size), me, device)
            return carry

        lax.fori_loop(1, size, step, 0, unroll=True)

    def whole(stage, group, target):
        size, me, device = groups[group]
        others = target(pl.ds(0, size - 1))
        return remote(stage, others, others, 0, 0, device(lax.rem(me + 1, size)))

    def send(stage, group, source, target):
        def start(p, me, device):
            remote(stage, source(p), target(me), 0, 0, device(p)).start()

        each(group, start)
        pending.append(lambda: whole(stage, group, target).wait_send())

    def receive(stage, group, target):
        whole(stage, group, target).wait_recv()

    weights = r["weights"]
    load = pltpu.make_async_copy(w_hbm, weights, r["load_sem"])
    load.start()
    barrier = pltpu.get_barrier_semaphore()
    for group in ("a", "b"):
        each(
            group,
            lambda p, me, device: pl.semaphore_signal(
                barrier, inc=1, device_id=device(p), device_id_type=MESH
            ),
        )
    feats_y = r["feats_y"]
    feats_y[y] = feats[...]

    perm = r["perm"]
    log_a, log_b = n_a.bit_length() - 1, n_b.bit_length() - 1
    line = iota((rows, rows), 0)
    from_row = (
        jnp.bitwise_and(line >> 1, n_a - 1) * (2 * n_b)
        + (line >> (1 + log_a)) * 2
        + jnp.bitwise_and(line, 1)
    )
    perm[...] = jnp.where(from_row == iota((rows, rows), 1), 1.0, 0.0).astype(BF16)

    def first(name, forward):
        group, size = ("a", n_a) if forward else ("b", n_b)
        source, target = r[name + "_s1"], r[name + "_r1"]
        me = groups[group][1]
        send(name + group, group, lambda p: source.at[p], lambda m: target.at[m])
        target[me] = source[me]

    def second(name, forward):
        group, size = ("a", n_a) if forward else ("b", n_b)
        other, other_size = ("b", n_b) if forward else ("a", n_a)
        middle = r[name + "_r1"]
        receive(name + group, group, lambda p: middle.at[p])
        source, target = r[name + "_s2"], r[name + "_r2"]
        lanes = middle.shape[2]
        moved = nn(perm[...], middle[...].reshape(rows, lanes)).astype(BF16)
        source[...] = moved.reshape(other_size, rows // other_size, lanes)
        me = groups[other][1]
        send(name + other, other, lambda p: source.at[p], lambda m: target.at[m])
        target[me] = source[me]

    def third(name, forward):
        other = "b" if forward else "a"
        target = r[name + "_r2"]
        receive(name + other, other, lambda p: target.at[p])
        return target

    counts = r["counts"][...].astype(F32)
    tails = r["tails"][...].astype(F32)
    triangle = jnp.where(iota((q_dev, q_dev), 0) <= iota((q_dev, q_dev), 1), 1.0, 0.0)
    ends = nn(jnp.broadcast_to(counts, (8, q_dev)).astype(BF16), triangle.astype(BF16))[0:1]
    starts = ends - counts
    pos = iota((slots, q_dev), 0).astype(F32)
    member = jnp.logical_and(pos < ends, pos >= starts)
    used = jnp.where(pos == ends - 1.0, tails, float(BLK))
    slot_used = jnp.sum(jnp.where(member, used, 0.0), axis=1, keepdims=True)
    valid = iota((slots, BLK), 1).astype(F32) < slot_used
    n_cand = (counts - 1.0) * BLK + tails
    logit = r["teacher"][...].astype(F32)
    top = jnp.max(jnp.where(valid, logit, -1e30), axis=1, keepdims=True)
    query_top = jnp.max(jnp.where(member, top, -1e30), axis=0, keepdims=True)
    slot_top = jnp.sum(jnp.where(member, query_top, 0.0), axis=1, keepdims=True)
    expo = jnp.where(valid, jnp.exp(logit - slot_top), 0.0)
    slot_sum = jnp.sum(expo, axis=1, keepdims=True)
    total = jnp.sum(jnp.where(member, slot_sum, 0.0), axis=0, keepdims=True)
    query_shift = query_top + jnp.log(total / n_cand)
    slot_shift = jnp.sum(jnp.where(member, query_shift, 0.0), axis=1, keepdims=True)
    diagonal = iota((slots, slots), 0) == iota((slots, slots), 1)
    owner_row = r["owner"][...]
    owner = jnp.sum(
        jnp.where(diagonal, owner_row.astype(F32), 0.0), axis=1, keepdims=True
    ).astype(I32)
    block = jnp.sum(
        jnp.where(diagonal, r["block"][...].astype(F32), 0.0), axis=1, keepdims=True
    )
    same = jnp.logical_and(
        owner_row == owner, iota((slots, slots), 1) < iota((slots, slots), 0)
    )
    rank = jnp.sum(jnp.where(same, 1.0, 0.0), axis=1, keepdims=True)
    log_y, log_x = n_y.bit_length() - 1, n_x.bit_length() - 1
    owner_y = jnp.bitwise_and(owner, n_y - 1)
    owner_core = jnp.bitwise_and(owner >> log_y, 1)
    owner_x = jnp.bitwise_and(owner >> (log_y + 1), n_x - 1)
    owner_z = owner >> (log_y + 1 + log_x)
    base = ((owner_x * n_y + owner_y) * n_b + owner_z * 2 + owner_core) * CAP
    dest = base.astype(F32) + rank
    place = jnp.where(dest == iota((slots, rows), 1).astype(F32), 1.0, 0.0).astype(BF16)
    side = in_lanes((block, slot_used) + pieces(slot_shift), slots)
    payload = jnp.concatenate([logit, side], axis=1).astype(BF16)
    placed = tn(place, payload).astype(BF16)
    r["e1_s1"][...] = nn(perm[...], placed).astype(BF16).reshape(r["e1_s1"].shape)
    member_row = r["member_row"]
    member_row[...] = tn(place, jnp.where(member, 1.0, 0.0).astype(BF16))
    pl.semaphore_wait(barrier, n_a + n_b - 2)
    send("feats", "y", lambda p: feats, lambda me: feats_y.at[me])
    first("e1", False)
    second("e1", False)

    receive("feats", "y", lambda p: feats_y.at[p])
    load.wait()
    preact, preact_x = r["preact"], r["preact_x"]
    group_rows = n_y * q_dev
    everyone = feats_y[...].reshape(group_rows, depth)
    step_units = min(256, units)

    def forward(j, total_emb):
        columns = pl.ds(pl.multiple_of(j * step_units, step_units), step_units)
        part = nn(everyone, weights[:, columns])
        preact[:, columns] = part
        hidden = (part / (1.0 + jnp.exp(-part))).astype(BF16)
        return total_emb + nn(hidden, w_embed[columns, :])

    emb_part = lax.fori_loop(
        0, units // step_units, forward, jnp.zeros((group_rows, emb), F32)
    )
    emb_s, emb_r = r["emb_s"], r["emb_r"]
    emb_s[...] = emb_part.reshape(n_y, q_dev, emb)
    send("emb", "y", lambda p: emb_s.at[p], lambda me: emb_r.at[me])
    emb_r[y] = emb_s[y]

    chunks = max(1, rows // 128)
    per = n_b // chunks
    chunk_rows = rows // chunks

    def lift(values, block_in):
        parts = [jnp.where(block_in == float(k), values, 0.0).astype(BF16) for k in range(BLK_DEV)]
        return jnp.concatenate(parts, axis=1)

    sent = r["e1_q"]
    by_owner = third("e1", False)[...].reshape(rows, 2 * BLK)
    sent[...] = nn(perm[...], by_owner).astype(BF16).reshape(sent.shape)
    teacher_n, info, spread = r["teacher_n"], r["info"], r["spread"]

    def chunk_of(ref, j):
        return ref[pl.ds(j * per, per)].reshape(chunk_rows, ref.shape[2])

    def rows_of(j):
        return pl.ds(pl.multiple_of(j * chunk_rows, chunk_rows), chunk_rows)

    def teacher_part(j, carry):
        chunk = chunk_of(sent, j).astype(F32)
        notes = chunk[:, BLK : 2 * BLK]
        block_in, used_in = notes[:, 0:1], notes[:, 1:2]
        shift_in = notes[:, 2:3] + notes[:, 3:4] + notes[:, 4:5]
        valid_in = iota((chunk_rows, BLK), 1).astype(F32) < used_in
        probs = jnp.where(valid_in, jnp.exp(chunk[:, :BLK] - shift_in), 0.0)
        teacher_n[rows_of(j), :] = probs
        info[rows_of(j), :] = notes
        term = nn(lift(probs, block_in), items[...])
        r["e2_s1"][pl.ds(j * per, per)] = term.astype(BF16).reshape(per, 2 * n_a, emb)
        return carry

    lax.fori_loop(0, chunks, teacher_part, 0)
    first("e2", False)

    receive("emb", "y", lambda p: emb_r.at[p])
    emb_raw = jnp.sum(emb_r[...], axis=0)
    inv_rms = lax.rsqrt(jnp.mean(emb_raw * emb_raw, axis=1, keepdims=True) + EPS)
    query_emb = (emb_raw * inv_rms).astype(BF16)
    member_bf = member_row[...].astype(BF16)
    r["e3_s1"][...] = nn(member_bf, query_emb).astype(BF16).reshape(r["e3_s1"].shape)
    first("e3", True)

    second("e2", False)
    second("e3", True)
    preact_x[x] = preact[...].astype(BF16)
    feats_s, feats_x = r["feats_s"], r["feats_x"]
    for p in range(n_x):
        for k in range(n_z):
            column = (k * n_x + p) * block_cols
            feats_s[p, :, k * block_cols : (k + 1) * block_cols] = feats_y[
                :, :, column : column + block_cols
            ].reshape(group_rows, block_cols)
    send("px", "x", lambda p: preact_x.at[x], lambda me: preact_x.at[me])
    send("fx", "x", lambda p: feats_s.at[p], lambda me: feats_x.at[me])
    feats_x[x] = feats_s[x]

    queries = third("e3", True)
    scores = r["scores"]

    e4_s, e4_r = r["e4_s1"], r["e4_r1"]

    def score_part(turn, carry):
        j = lax.rem(turn + b // per + 1, chunks)
        every = nt(chunk_of(queries, j), items[...])
        notes = info[rows_of(j), :]
        block_in, used_in = notes[:, 0:1], notes[:, 1:2]
        picked = jnp.zeros((chunk_rows, BLK), F32)
        for k in range(BLK_DEV):
            picked = jnp.where(block_in == float(k), every[:, k * BLK : (k + 1) * BLK], picked)
        valid_in = iota((chunk_rows, BLK), 1).astype(F32) < used_in
        row_top = jnp.max(jnp.where(valid_in, picked, -1e30), axis=1, keepdims=True)
        row_expo = jnp.where(valid_in, jnp.exp(picked - row_top), 0.0)
        row_sum = jnp.maximum(jnp.sum(row_expo, axis=1, keepdims=True), 1e-30)
        scores[rows_of(j), :] = picked
        term = nn(lift(row_expo / row_sum, block_in), items[...])
        empty = used_in < 0.5
        lse = jnp.where(empty, 0.0, row_top + jnp.log(row_sum))
        message = jnp.concatenate([term, in_lanes(pieces(lse), chunk_rows)], axis=1)
        e4_s[pl.ds(j * per, per)] = message.astype(BF16).reshape(per, 2 * n_a, emb + 128)
        for i in range(per):
            p = j * per + i

            @pl.when(p != b)
            def _():
                remote("e4b", e4_s.at[p], e4_r.at[b], 0, 0, groups["b"][2](p)).start()

        return carry

    lax.fori_loop(0, chunks, score_part, 0)
    pending.append(lambda: whole("e4b", "b", lambda p: e4_r.at[p]).wait_send())
    e4_r[b] = e4_s[b]
    second("e4", False)
    back = third("e2", False)
    query_teacher = tn(member_bf, back[...].reshape(rows, emb))
    returned = third("e4", False)[...].reshape(rows, emb + 128)

    lse_bits = returned[:, emb : emb + 128].astype(F32)
    lse_in = lse_bits[:, 0:1] + lse_bits[:, 1:2] + lse_bits[:, 2:3]
    mine = member_row[...] > 0.5
    query_max = jnp.max(jnp.where(mine, lse_in, -1e30), axis=0, keepdims=True)
    weight = jnp.where(mine, jnp.exp(lse_in - query_max), 0.0)
    scale = n_cand / jnp.sum(weight, axis=0, keepdims=True)
    weight = weight * scale
    weight_high = weight.astype(BF16)
    weight_low = (weight - weight_high.astype(F32)).astype(BF16)
    mean_item = returned[:, :emb]
    gradient = tn(weight_high, mean_item) + tn(weight_low, mean_item) - query_teacher
    grad_emb = (
        inv_rms
        * (
            gradient
            - emb_raw * inv_rms * inv_rms * jnp.mean(gradient * emb_raw, axis=1, keepdims=True)
        )
    ).astype(BF16)
    grad_a = r["grad_a"]
    grad_a[a] = grad_emb
    send("ga", "a", lambda p: grad_a.at[a], lambda me: grad_a.at[me])
    shift = query_max - jnp.log(scale)
    row_shift = jnp.sum(jnp.where(mine, shift, 0.0), axis=1, keepdims=True)
    r["e5_s1"][...] = in_lanes(pieces(row_shift), rows).astype(BF16).reshape(r["e5_s1"].shape)
    first("e5", True)
    def derivative(dhidden, before):
        sig = 1.0 / (1.0 + jnp.exp(-before))
        return (dhidden * sig * (1.0 + before * (1.0 - sig))).astype(BF16)

    receive("px", "x", lambda p: preact_x.at[p])
    receive("fx", "x", lambda p: feats_x.at[p])
    receive("ga", "a", lambda p: grad_a.at[p])
    grad_group = grad_a[pl.ds(x * n_y, n_y)].reshape(group_rows, emb)

    pre_x = r["pre_x"]

    def pre_part(j, carry):
        part = grad_a[pl.ds(j * n_y, n_y)].reshape(group_rows, emb)
        pre_x[j] = derivative(nt(part, w_embed[...]), preact_x[j].astype(F32))
        return carry

    lax.fori_loop(0, n_x, pre_part, 0)
    line_rows = n_x * group_rows

    part_units = units // n_x
    mine_units = pl.ds(pl.multiple_of(x * part_units, part_units), part_units)
    before = preact_x[:, :, mine_units].astype(F32).reshape(line_rows, part_units)
    hidden_x = (before / (1.0 + jnp.exp(-before))).astype(BF16)
    er_s, er_r, eb, ex = r["er_s"], r["er_r"], r["eb"], r["ex"]
    er_s[...] = tn(hidden_x, grad_a[...].reshape(line_rows, emb)).astype(BF16).reshape(er_s.shape)
    send("er", "b", lambda p: er_s.at[p], lambda me: er_r.at[me])
    er_r[b] = er_s[b]

    halves, halves_bf, core_r = r["halves"], r["halves_bf"], r["core_r"]
    z_s, z_r = r["z_s"], r["z_r"]
    mate = at(z, x, 1 - core, y)

    def core_copy(k):
        return remote("core", halves_bf.at[k, 1 - core], core_r.at[k], 0, k, mate)

    def z_copy(k):
        return remote("zs", z_s.at[k], z_r.at[z], 0, 0, at(k, x, core, y))

    def block_at(j):
        return lax.rem(z + n_z // 2 + j, n_z)

    def hidden_part(j):
        k = block_at(j)
        columns = pl.ds(pl.multiple_of(k * block_cols, block_cols), block_cols)
        left = feats_x[:, :, columns].reshape(line_rows, block_cols)
        value = tn(left, pre_x[...].reshape(line_rows, units)).reshape(2, half, units)
        halves[k] = value
        halves_bf[k] = value.astype(BF16)
        core_copy(k).start()

    def z_part(j):
        k = block_at(j)
        core_copy(k).wait_recv()
        z_s[k] = (halves[k, core] + core_r[k].astype(F32)).astype(BF16)

        @pl.when(k != z)
        def _():
            z_copy(k).start()

    lead = n_z // 2
    for j in range(lead):
        hidden_part(j)
    second("e5", True)
    receive("er", "b", lambda p: er_r.at[p])
    eb[b] = jnp.sum(er_r[...].astype(F32), axis=0).astype(BF16)
    send("eb", "b", lambda p: eb.at[b], lambda me: eb.at[me])

    def both_parts(j, carry):
        z_part(j)
        hidden_part(j + lead)
        return carry

    lax.fori_loop(0, n_z - lead, both_parts, 0)
    lax.fori_loop(n_z - lead, n_z, lambda j, carry: (z_part(j), carry)[1], 0)
    pending.append(
        lambda: remote("core", core_r, core_r, 0, 0, mate).wait_send()
    )
    pending.append(lambda: whole("zs", "z", lambda p: z_r.at[p]).wait_send())
    own = halves[z, core] + core_r[z].astype(F32)

    grad_pre = derivative(nt(grad_group, w_embed[...]), preact[...])
    gf_s, gf_r = r["gf_s"], r["gf_r"]
    step_depth = min(256, depth // 4)

    def feats_part(part):
        quarter = depth // 4

        def step(j, carry):
            start = pl.multiple_of(part * quarter + j * step_depth, step_depth)
            value = nt(grad_pre, weights[pl.ds(start, step_depth), :])
            gf_s[:, :, pl.ds(start, step_depth)] = value.astype(BF16).reshape(
                n_y, q_dev, step_depth
            )
            return carry

        lax.fori_loop(0, quarter // step_depth, step, 0)
        columns = pl.ds(part * quarter, quarter)
        send(
            "gf" + str(part),
            "y",
            lambda p: gf_s.at[p, :, columns],
            lambda me: gf_r.at[me, :, columns],
        )
    for part in range(4):
        feats_part(part)
    receive("eb", "b", lambda p: eb.at[p])
    ex[x] = eb[...].reshape(part_units, emb)
    send("ex", "x", lambda p: ex.at[x], lambda me: ex.at[me])

    shifts = third("e5", True)

    def item_part(j, carry):
        notes = info[rows_of(j), :]
        block_in, used_in = notes[:, 0:1], notes[:, 1:2]
        bits = chunk_of(shifts, j).astype(F32)
        shift_in = bits[:, 0:1] + bits[:, 1:2] + bits[:, 2:3]
        valid_in = iota((chunk_rows, BLK), 1).astype(F32) < used_in
        student = jnp.where(valid_in, jnp.exp(scores[rows_of(j), :] - shift_in), 0.0)
        spread[rows_of(j), :] = lift(student - teacher_n[rows_of(j), :], block_in)
        return carry

    lax.fori_loop(0, chunks, item_part, 0)

    def item_block(j, carry):
        columns = pl.ds(pl.multiple_of(j * 256, 256), 256)
        r["grad_items"][columns, :] = tn(
            spread[:, columns], queries[...].reshape(rows, emb)
        )
        return carry

    lax.fori_loop(0, BLK_DEV * BLK // 256, item_block, 0)
    for part in range(4):
        columns = pl.ds(part * (depth // 4), depth // 4)
        receive("gf" + str(part), "y", lambda p: gf_r.at[p, :, columns])
    gf_r[y] = gf_s[y]
    r["grad_feats"][...] = jnp.sum(gf_r[...].astype(F32), axis=0)
    receive("ex", "x", lambda p: ex.at[p])
    r["grad_embed"][...] = ex[...].astype(F32).reshape(units, emb)
    receive("zs", "z", lambda p: z_r.at[p])
    z_r[z] = jnp.zeros((half, units), BF16)
    r["grad_hidden"][...] = own + jnp.sum(z_r[...].astype(F32), axis=0)
    for finish in pending:
        finish()


def hand_on(*refs):
    count = (len(refs) - 2) // 3
    sources, targets, buffers = refs[:count], refs[count : 2 * count], refs[2 * count : 3 * count]
    load_sem, store_sem = refs[-2:]
    loads = [
        pltpu.make_async_copy(sources[k], buffers[k], load_sem.at[k]) for k in range(count)
    ]
    stores = [
        pltpu.make_async_copy(buffers[k], targets[k], store_sem.at[k]) for k in range(count)
    ]
    for load in loads:
        load.start()
    for load, store in zip(loads, stores):
        load.wait()
        store.start()
    for store in stores:
        store.wait()


def per_device(
    n_z, n_x, n_y, feats, w_hidden, w_embed, items, teacher, block_counts, tail_rows,
    cand_owner, cand_block,
):
    q_dev, depth = feats.shape
    units, emb = w_embed.shape
    slots = cand_owner.shape[0]
    n_a, n_b = n_x * n_y, n_z * 2
    rows = n_a * n_b * CAP
    group_rows = n_y * q_dev
    block_cols = depth // (n_z * n_x)
    half = block_cols // 2
    part_units = units // n_x
    inputs = {
        "feats": feats,
        "w_hidden": w_hidden,
        "w_embed": w_embed,
        "items": items,
        "teacher": teacher,
        "counts": block_counts,
        "tails": tail_rows.reshape(1, q_dev),
        "owner": cand_owner.reshape(1, slots),
        "block": cand_block.reshape(1, slots),
    }
    outputs = {
        "grad_feats": (q_dev, depth),
        "grad_hidden": (half, units),
        "grad_embed": (units, emb),
        "grad_items": (BLK_DEV * BLK, emb),
    }
    vmem = {
        "weights": ((depth, units), BF16),
        "feats_y": ((n_y, q_dev, depth), BF16),
        "perm": ((rows, rows), BF16),
        "member_row": ((rows, q_dev), F32),
        "preact": ((group_rows, units), F32),
        "preact_x": ((n_x, group_rows, units), BF16),
        "emb_s": ((n_y, q_dev, emb), F32),
        "emb_r": ((n_y, q_dev, emb), F32),
        "teacher_n": ((rows, BLK), F32),
        "info": ((rows, 128), F32),
        "spread": ((rows, BLK_DEV * BLK), BF16),
        "feats_s": ((n_x, group_rows, n_z * block_cols), BF16),
        "feats_x": ((n_x, group_rows, n_z * block_cols), BF16),
        "scores": ((rows, BLK), F32),
        "e1_q": ((n_b, 2 * n_a, 2 * BLK), BF16),
        "grad_a": ((n_a, q_dev, emb), BF16),
        "gf_s": ((n_y, q_dev, depth), BF16),
        "gf_r": ((n_y, q_dev, depth), BF16),
        "pre_x": ((n_x, group_rows, units), BF16),
        "halves": ((n_z, 2, half, units), F32),
        "halves_bf": ((n_z, 2, half, units), BF16),
        "core_r": ((n_z, half, units), BF16),
        "z_s": ((n_z, half, units), BF16),
        "z_r": ((n_z, half, units), BF16),
        "er_s": ((n_b, part_units // n_b, emb), BF16),
        "er_r": ((n_b, part_units // n_b, emb), BF16),
        "eb": ((n_b, part_units // n_b, emb), BF16),
        "ex": ((n_x, part_units, emb), BF16),
    }
    for name, lanes, ahead in (
        ("e1", 256, False),
        ("e2", emb, False),
        ("e3", emb, True),
        ("e4", emb + 128, False),
        ("e5", 128, True),
    ):
        one, two = ((n_a, 2 * n_b, lanes), (n_b, 2 * n_a, lanes))
        if not ahead:
            one, two = two, one
        for suffix, shape in (("_s1", one), ("_r1", one), ("_s2", two), ("_r2", two)):
            vmem[name + suffix] = (shape, BF16)
    scratch = [pltpu.VMEM(shape, kind) for shape, kind in vmem.values()]
    most = max(n_a, n_b)
    scratch += [
        pltpu.SemaphoreType.DMA((len(STAGES), most)),
        pltpu.SemaphoreType.DMA((len(STAGES), most)),
        pltpu.SemaphoreType.DMA,
    ]
    names = list(inputs) + list(outputs) + list(vmem) + ["send_sem", "recv_sem", "load_sem"]
    specs = [
        pl.BlockSpec(memory_space=pl.ANY if name == "w_hidden" else pltpu.VMEM)
        for name in inputs
    ]
    results = pl.pallas_call(
        functools.partial(kernel, n_z, n_x, n_y, names),
        out_shape=[jax.ShapeDtypeStruct(shape, F32) for shape in outputs.values()],
        in_specs=specs,
        out_specs=[pl.BlockSpec(memory_space=pltpu.VMEM)] * len(outputs),
        scratch_shapes=scratch,
        compiler_params=pltpu.CompilerParams(
            collective_id=0, has_side_effects=True, vmem_limit_bytes=58 * 1024 * 1024
        ),
    )(*inputs.values())
    return pl.pallas_call(
        hand_on,
        out_shape=[jax.ShapeDtypeStruct(shape, F32) for shape in outputs.values()],
        in_specs=[pl.BlockSpec(memory_space=pl.ANY)] * len(outputs),
        out_specs=[pl.BlockSpec(memory_space=pl.ANY)] * len(outputs),
        scratch_shapes=[pltpu.VMEM(shape, F32) for shape in outputs.values()]
        + [pltpu.SemaphoreType.DMA((len(outputs),))] * 2,
    )(*results)


def solution(mesh):
    n_y = mesh.shape["sub"]
    n_x = n_y
    n_z = mesh.shape["shard"] // (2 * n_x)
    both = ("shard", "sub")
    placed = (
        P(both, None),
        P(None, "sub"),
        P("sub", None),
        P(both, None),
        P(both, None),
        P(both, None),
        P(both),
        P(both, None),
        P(both),
    )
    return jax.shard_map(
        functools.partial(per_device, n_z, n_x, n_y),
        mesh=mesh,
        in_specs=placed,
        out_specs=(P(both, None), P("shard", "sub"), P("sub", None), P(both, None)),
        check_vma=False,
    )
```

```python
import functools

import jax
import jax.numpy as jnp
from jax import lax
from jax.experimental import pallas as pl
from jax.experimental.pallas import tpu as pltpu
from jax.sharding import PartitionSpec as P

BLK = 128
BLK_DEV = 8
CAP = 2
EPS = 1e-06
F32 = jnp.float32
BF16 = jnp.bfloat16
I32 = jnp.int32
MESH = pl.DeviceIdType.MESH
STAGES = (
    "feats", "emb", "e1a", "e1b", "e2b", "e2a", "e3a", "e3b", "e4b", "e4a", "e5a", "e5b",
    "px", "fx", "ga", "core", "zs", "gf0", "gf1", "gf2", "gf3", "er", "eb", "ex",
)


def dot(left, right, left_dim, right_dim):
    return lax.dot_general(
        left, right, (((left_dim,), (right_dim,)), ((), ())), preferred_element_type=F32
    )


def nn(left, right):
    return dot(left, right, 1, 0)


def tn(left, right):
    return dot(left, right, 0, 0)


def nt(left, right):
    return dot(left, right, 1, 1)


def iota(shape, axis):
    return lax.broadcasted_iota(I32, shape, axis)


def pieces(value):
    high = value.astype(BF16).astype(F32)
    rest = value - high
    middle = rest.astype(BF16).astype(F32)
    return high, middle, rest - middle


def in_lanes(columns, rows):
    lane = iota((rows, 128), 1)
    result = jnp.zeros((rows, 128), F32)
    for place, column in enumerate(columns):
        result = jnp.where(lane == place, column, result)
    return result


def kernel(n_z, n_x, n_y, names, *refs):
    r = dict(zip(names, refs))
    feats, w_hbm = r["feats"], r["w_hidden"]
    w_embed, items = r["w_embed_v"], r["items_v"]
    n_a, n_b = n_x * n_y, n_z * 2
    rows = n_a * n_b * CAP
    q_dev, depth = feats.shape
    units = w_hbm.shape[1]
    emb = w_embed.shape[1]
    slots = r["teacher"].shape[0]
    block_cols = depth // (n_z * n_x)
    half = block_cols // 2

    shard, y = lax.axis_index("shard"), lax.axis_index("sub")
    core = lax.rem(shard, 2)
    x = lax.rem(shard // 2, n_x)
    z = shard // (2 * n_x)
    a = x * n_y + y
    b = z * 2 + core

    def at(z_, x_, core_, y_):
        return ((z_ * n_x + x_) * 2 + core_, y_)

    groups = {
        "y": (n_y, y, lambda p: at(z, x, core, p)),
        "x": (n_x, x, lambda p: at(z, p, core, y)),
        "z": (n_z, z, lambda p: at(p, x, core, y)),
        "a": (n_a, a, lambda p: at(z, p // n_y, core, lax.rem(p, n_y))),
        "b": (n_b, b, lambda p: at(p // 2, x, lax.rem(p, 2), y)),
    }
    send_sem, recv_sem = r["send_sem"], r["recv_sem"]
    pending = []

    def remote(stage, source, target, send_at, recv_at, device):
        row = STAGES.index(stage)
        return pltpu.make_async_remote_copy(
            src_ref=source,
            dst_ref=target,
            send_sem=send_sem.at[row, send_at],
            recv_sem=recv_sem.at[row, recv_at],
            device_id=device,
            device_id_type=MESH,
        )

    def each(group, body):
        size, me, device = groups[group]

        def step(j, carry):
            body(lax.rem(me + j, size), me, device)
            return carry

        lax.fori_loop(1, size, step, 0, unroll=True)

    def whole(stage, group, target):
        size, me, device = groups[group]
        others = target(pl.ds(0, size - 1))
        return remote(stage, others, others, 0, 0, device(lax.rem(me + 1, size)))

    def send(stage, group, source, target):
        def start(p, me, device):
            remote(stage, source(p), target(me), 0, 0, device(p)).start()

        each(group, start)
        pending.append(lambda: whole(stage, group, target).wait_send())

    def receive(stage, group, target):
        whole(stage, group, target).wait_recv()

    weights = r["weights"]
    barrier = pltpu.get_barrier_semaphore()
    for group in ("a", "b"):
        each(
            group,
            lambda p, me, device: pl.semaphore_signal(
                barrier, inc=1, device_id=device(p), device_id_type=MESH
            ),
        )
    feats_y = r["feats_y"]
    loads = [
        pltpu.make_async_copy(source, target, r["load_sem"].at[k])
        for k, (source, target) in enumerate(
            (
                (feats, feats_y.at[y]),
                (w_hbm, weights),
                (r["w_embed"], w_embed),
                (r["items"], items),
            )
        )
    ]
    for load in loads:
        load.start()

    perm = r["perm"]
    log_a, log_b = n_a.bit_length() - 1, n_b.bit_length() - 1
    line = iota((rows, rows), 0)
    from_row = (
        jnp.bitwise_and(line >> 1, n_a - 1) * (2 * n_b)
        + (line >> (1 + log_a)) * 2
        + jnp.bitwise_and(line, 1)
    )
    perm[...] = jnp.where(from_row == iota((rows, rows), 1), 1.0, 0.0).astype(BF16)

    def first(name, forward):
        group, size = ("a", n_a) if forward else ("b", n_b)
        source, target = r[name + "_s1"], r[name + "_r1"]
        me = groups[group][1]
        send(name + group, group, lambda p: source.at[p], lambda m: target.at[m])
        target[me] = source[me]

    def second(name, forward):
        group, size = ("a", n_a) if forward else ("b", n_b)
        other, other_size = ("b", n_b) if forward else ("a", n_a)
        middle = r[name + "_r1"]
        receive(name + group, group, lambda p: middle.at[p])
        source, target = r[name + "_s2"], r[name + "_r2"]
        lanes = middle.shape[2]
        moved = nn(perm[...], middle[...].reshape(rows, lanes)).astype(BF16)
        source[...] = moved.reshape(other_size, rows // other_size, lanes)
        me = groups[other][1]
        send(name + other, other, lambda p: source.at[p], lambda m: target.at[m])
        target[me] = source[me]

    def third(name, forward):
        other = "b" if forward else "a"
        target = r[name + "_r2"]
        receive(name + other, other, lambda p: target.at[p])
        return target

    counts = r["counts"][...].astype(F32)
    tails = r["tails"][...].astype(F32)
    triangle = jnp.where(iota((q_dev, q_dev), 0) <= iota((q_dev, q_dev), 1), 1.0, 0.0)
    ends = nn(jnp.broadcast_to(counts, (8, q_dev)).astype(BF16), triangle.astype(BF16))[0:1]
    starts = ends - counts
    pos = iota((slots, q_dev), 0).astype(F32)
    member = jnp.logical_and(pos < ends, pos >= starts)
    used = jnp.where(pos == ends - 1.0, tails, float(BLK))
    slot_used = jnp.sum(jnp.where(member, used, 0.0), axis=1, keepdims=True)
    valid = iota((slots, BLK), 1).astype(F32) < slot_used
    n_cand = (counts - 1.0) * BLK + tails
    logit = r["teacher"][...].astype(F32)
    top = jnp.max(jnp.where(valid, logit, -1e30), axis=1, keepdims=True)
    query_top = jnp.max(jnp.where(member, top, -1e30), axis=0, keepdims=True)
    slot_top = jnp.sum(jnp.where(member, query_top, 0.0), axis=1, keepdims=True)
    expo = jnp.where(valid, jnp.exp(logit - slot_top), 0.0)
    slot_sum = jnp.sum(expo, axis=1, keepdims=True)
    total = jnp.sum(jnp.where(member, slot_sum, 0.0), axis=0, keepdims=True)
    query_shift = query_top + jnp.log(total / n_cand)
    slot_shift = jnp.sum(jnp.where(member, query_shift, 0.0), axis=1, keepdims=True)
    diagonal = iota((slots, slots), 0) == iota((slots, slots), 1)
    owner_row = r["owner"][...]
    owner = jnp.sum(
        jnp.where(diagonal, owner_row.astype(F32), 0.0), axis=1, keepdims=True
    ).astype(I32)
    block = jnp.sum(
        jnp.where(diagonal, r["block"][...].astype(F32), 0.0), axis=1, keepdims=True
    )
    same = jnp.logical_and(
        owner_row == owner, iota((slots, slots), 1) < iota((slots, slots), 0)
    )
    rank = jnp.sum(jnp.where(same, 1.0, 0.0), axis=1, keepdims=True)
    log_y, log_x = n_y.bit_length() - 1, n_x.bit_length() - 1
    owner_y = jnp.bitwise_and(owner, n_y - 1)
    owner_core = jnp.bitwise_and(owner >> log_y, 1)
    owner_x = jnp.bitwise_and(owner >> (log_y + 1), n_x - 1)
    owner_z = owner >> (log_y + 1 + log_x)
    base = ((owner_x * n_y + owner_y) * n_b + owner_z * 2 + owner_core) * CAP
    dest = base.astype(F32) + rank
    place = jnp.where(dest == iota((slots, rows), 1).astype(F32), 1.0, 0.0).astype(BF16)
    side = in_lanes((block, slot_used) + pieces(slot_shift), slots)
    payload = jnp.concatenate([logit, side], axis=1).astype(BF16)
    placed = tn(place, payload).astype(BF16)
    r["e1_s1"][...] = nn(perm[...], placed).astype(BF16).reshape(r["e1_s1"].shape)
    member_row = r["member_row"]
    member_row[...] = tn(place, jnp.where(member, 1.0, 0.0).astype(BF16))
    pl.semaphore_wait(barrier, n_a + n_b - 2)
    send("feats", "y", lambda p: feats, lambda me: feats_y.at[me])
    first("e1", False)
    second("e1", False)

    receive("feats", "y", lambda p: feats_y.at[p])
    for load in loads:
        load.wait()
    preact, preact_x = r["preact"], r["preact_x"]
    group_rows = n_y * q_dev
    everyone = feats_y[...].reshape(group_rows, depth)
    step_units = min(256, units)

    def forward(j, total_emb):
        columns = pl.ds(pl.multiple_of(j * step_units, step_units), step_units)
        part = nn(everyone, weights[:, columns])
        preact[:, columns] = part
        hidden = (part / (1.0 + jnp.exp(-part))).astype(BF16)
        return total_emb + nn(hidden, w_embed[columns, :])

    emb_part = lax.fori_loop(
        0, units // step_units, forward, jnp.zeros((group_rows, emb), F32)
    )
    emb_s, emb_r = r["emb_s"], r["emb_r"]
    emb_s[...] = emb_part.reshape(n_y, q_dev, emb)
    send("emb", "y", lambda p: emb_s.at[p], lambda me: emb_r.at[me])
    emb_r[y] = emb_s[y]

    chunks = max(1, rows // 128)
    per = n_b // chunks
    chunk_rows = rows // chunks

    def lift(values, block_in):
        parts = [jnp.where(block_in == float(k), values, 0.0).astype(BF16) for k in range(BLK_DEV)]
        return jnp.concatenate(parts, axis=1)

    sent = r["e1_q"]
    by_owner = third("e1", False)[...].reshape(rows, 2 * BLK)
    sent[...] = nn(perm[...], by_owner).astype(BF16).reshape(sent.shape)
    teacher_n, info, spread = r["teacher_n"], r["info"], r["spread"]

    def chunk_of(ref, j):
        return ref[pl.ds(j * per, per)].reshape(chunk_rows, ref.shape[2])

    def rows_of(j):
        return pl.ds(pl.multiple_of(j * chunk_rows, chunk_rows), chunk_rows)

    def teacher_part(j, carry):
        chunk = chunk_of(sent, j).astype(F32)
        notes = chunk[:, BLK : 2 * BLK]
        block_in, used_in = notes[:, 0:1], notes[:, 1:2]
        shift_in = notes[:, 2:3] + notes[:, 3:4] + notes[:, 4:5]
        valid_in = iota((chunk_rows, BLK), 1).astype(F32) < used_in
        probs = jnp.where(valid_in, jnp.exp(chunk[:, :BLK] - shift_in), 0.0)
        teacher_n[rows_of(j), :] = probs
        info[rows_of(j), :] = notes
        term = nn(lift(probs, block_in), items[...])
        r["e2_s1"][pl.ds(j * per, per)] = term.astype(BF16).reshape(per, 2 * n_a, emb)
        return carry

    lax.fori_loop(0, chunks, teacher_part, 0)
    first("e2", False)

    receive("emb", "y", lambda p: emb_r.at[p])
    emb_raw = jnp.sum(emb_r[...], axis=0)
    inv_rms = lax.rsqrt(jnp.mean(emb_raw * emb_raw, axis=1, keepdims=True) + EPS)
    query_emb = (emb_raw * inv_rms).astype(BF16)
    member_bf = member_row[...].astype(BF16)
    r["e3_s1"][...] = nn(member_bf, query_emb).astype(BF16).reshape(r["e3_s1"].shape)
    first("e3", True)

    second("e2", False)
    second("e3", True)
    preact_x[x] = preact[...].astype(BF16)
    feats_s, feats_x = r["feats_s"], r["feats_x"]
    for p in range(n_x):
        for k in range(n_z):
            column = (k * n_x + p) * block_cols
            feats_s[p, :, k * block_cols : (k + 1) * block_cols] = feats_y[
                :, :, column : column + block_cols
            ].reshape(group_rows, block_cols)
    send("px", "x", lambda p: preact_x.at[x], lambda me: preact_x.at[me])
    send("fx", "x", lambda p: feats_s.at[p], lambda me: feats_x.at[me])
    feats_x[x] = feats_s[x]

    queries = third("e3", True)
    scores = r["scores"]

    e4_s, e4_r = r["e4_s1"], r["e4_r1"]

    def score_part(turn, carry):
        j = lax.rem(turn + b // per + 1, chunks)
        every = nt(chunk_of(queries, j), items[...])
        notes = info[rows_of(j), :]
        block_in, used_in = notes[:, 0:1], notes[:, 1:2]
        picked = jnp.zeros((chunk_rows, BLK), F32)
        for k in range(BLK_DEV):
            picked = jnp.where(block_in == float(k), every[:, k * BLK : (k + 1) * BLK], picked)
        valid_in = iota((chunk_rows, BLK), 1).astype(F32) < used_in
        row_top = jnp.max(jnp.where(valid_in, picked, -1e30), axis=1, keepdims=True)
        row_expo = jnp.where(valid_in, jnp.exp(picked - row_top), 0.0)
        row_sum = jnp.maximum(jnp.sum(row_expo, axis=1, keepdims=True), 1e-30)
        scores[rows_of(j), :] = picked
        term = nn(lift(row_expo / row_sum, block_in), items[...])
        empty = used_in < 0.5
        lse = jnp.where(empty, 0.0, row_top + jnp.log(row_sum))
        message = jnp.concatenate([term, in_lanes(pieces(lse), chunk_rows)], axis=1)
        e4_s[pl.ds(j * per, per)] = message.astype(BF16).reshape(per, 2 * n_a, emb + 128)
        for i in range(per):
            p = j * per + i

            @pl.when(p != b)
            def _():
                remote("e4b", e4_s.at[p], e4_r.at[b], 0, 0, groups["b"][2](p)).start()

        return carry

    lax.fori_loop(0, chunks, score_part, 0)
    pending.append(lambda: whole("e4b", "b", lambda p: e4_r.at[p]).wait_send())
    e4_r[b] = e4_s[b]
    second("e4", False)
    back = third("e2", False)
    query_teacher = tn(member_bf, back[...].reshape(rows, emb))
    returned = third("e4", False)[...].reshape(rows, emb + 128)

    lse_bits = returned[:, emb : emb + 128].astype(F32)
    lse_in = lse_bits[:, 0:1] + lse_bits[:, 1:2] + lse_bits[:, 2:3]
    mine = member_row[...] > 0.5
    query_max = jnp.max(jnp.where(mine, lse_in, -1e30), axis=0, keepdims=True)
    weight = jnp.where(mine, jnp.exp(lse_in - query_max), 0.0)
    scale = n_cand / jnp.sum(weight, axis=0, keepdims=True)
    weight = weight * scale
    weight_high = weight.astype(BF16)
    weight_low = (weight - weight_high.astype(F32)).astype(BF16)
    mean_item = returned[:, :emb]
    gradient = tn(weight_high, mean_item) + tn(weight_low, mean_item) - query_teacher
    grad_emb = (
        inv_rms
        * (
            gradient
            - emb_raw * inv_rms * inv_rms * jnp.mean(gradient * emb_raw, axis=1, keepdims=True)
        )
    ).astype(BF16)
    grad_a = r["grad_a"]
    grad_a[a] = grad_emb
    send("ga", "a", lambda p: grad_a.at[a], lambda me: grad_a.at[me])
    shift = query_max - jnp.log(scale)
    row_shift = jnp.sum(jnp.where(mine, shift, 0.0), axis=1, keepdims=True)
    r["e5_s1"][...] = in_lanes(pieces(row_shift), rows).astype(BF16).reshape(r["e5_s1"].shape)
    first("e5", True)
    def derivative(dhidden, before):
        sig = 1.0 / (1.0 + jnp.exp(-before))
        return (dhidden * sig * (1.0 + before * (1.0 - sig))).astype(BF16)

    receive("px", "x", lambda p: preact_x.at[p])
    receive("fx", "x", lambda p: feats_x.at[p])
    receive("ga", "a", lambda p: grad_a.at[p])
    grad_group = grad_a[pl.ds(x * n_y, n_y)].reshape(group_rows, emb)

    pre_x = r["pre_x"]

    def pre_part(j, carry):
        part = grad_a[pl.ds(j * n_y, n_y)].reshape(group_rows, emb)
        pre_x[j] = derivative(nt(part, w_embed[...]), preact_x[j].astype(F32))
        return carry

    lax.fori_loop(0, n_x, pre_part, 0)
    line_rows = n_x * group_rows

    part_units = units // n_x
    mine_units = pl.ds(pl.multiple_of(x * part_units, part_units), part_units)
    before = preact_x[:, :, mine_units].astype(F32).reshape(line_rows, part_units)
    hidden_x = (before / (1.0 + jnp.exp(-before))).astype(BF16)
    er_s, er_r, eb, ex = r["er_s"], r["er_r"], r["eb"], r["ex"]
    er_s[...] = tn(hidden_x, grad_a[...].reshape(line_rows, emb)).astype(BF16).reshape(er_s.shape)
    send("er", "b", lambda p: er_s.at[p], lambda me: er_r.at[me])
    er_r[b] = er_s[b]

    halves, halves_bf, core_r = r["halves"], r["halves_bf"], r["core_r"]
    z_s, z_r = r["z_s"], r["z_r"]
    mate = at(z, x, 1 - core, y)

    def core_copy(k):
        return remote("core", halves_bf.at[k, 1 - core], core_r.at[k], 0, k, mate)

    def z_copy(k):
        return remote("zs", z_s.at[k], z_r.at[z], 0, 0, at(k, x, core, y))

    def block_at(j):
        return lax.rem(z + n_z // 2 + j, n_z)

    def hidden_part(j):
        k = block_at(j)
        columns = pl.ds(pl.multiple_of(k * block_cols, block_cols), block_cols)
        left = feats_x[:, :, columns].reshape(line_rows, block_cols)
        value = tn(left, pre_x[...].reshape(line_rows, units)).reshape(2, half, units)
        halves[k] = value
        halves_bf[k] = value.astype(BF16)
        core_copy(k).start()

    def z_part(j):
        k = block_at(j)
        core_copy(k).wait_recv()
        z_s[k] = (halves[k, core] + core_r[k].astype(F32)).astype(BF16)

        @pl.when(k != z)
        def _():
            z_copy(k).start()

    lead = n_z // 2
    for j in range(lead):
        hidden_part(j)
    second("e5", True)
    receive("er", "b", lambda p: er_r.at[p])
    eb[b] = jnp.sum(er_r[...].astype(F32), axis=0).astype(BF16)
    send("eb", "b", lambda p: eb.at[b], lambda me: eb.at[me])

    def both_parts(j, carry):
        z_part(j)
        hidden_part(j + lead)
        return carry

    lax.fori_loop(0, n_z - lead, both_parts, 0)
    lax.fori_loop(n_z - lead, n_z, lambda j, carry: (z_part(j), carry)[1], 0)
    pending.append(
        lambda: remote("core", core_r, core_r, 0, 0, mate).wait_send()
    )
    pending.append(lambda: whole("zs", "z", lambda p: z_r.at[p]).wait_send())
    own = halves[z, core] + core_r[z].astype(F32)

    grad_pre = derivative(nt(grad_group, w_embed[...]), preact[...])
    gf_s, gf_r = r["gf_s"], r["gf_r"]
    step_depth = min(256, depth // 4)

    def feats_part(part):
        quarter = depth // 4

        def step(j, carry):
            start = pl.multiple_of(part * quarter + j * step_depth, step_depth)
            value = nt(grad_pre, weights[pl.ds(start, step_depth), :])
            gf_s[:, :, pl.ds(start, step_depth)] = value.astype(BF16).reshape(
                n_y, q_dev, step_depth
            )
            return carry

        lax.fori_loop(0, quarter // step_depth, step, 0)
        columns = pl.ds(part * quarter, quarter)
        send(
            "gf" + str(part),
            "y",
            lambda p: gf_s.at[p, :, columns],
            lambda me: gf_r.at[me, :, columns],
        )
    for part in range(4):
        feats_part(part)
    receive("eb", "b", lambda p: eb.at[p])
    ex[x] = eb[...].reshape(part_units, emb)
    send("ex", "x", lambda p: ex.at[x], lambda me: ex.at[me])

    shifts = third("e5", True)

    def item_part(j, carry):
        notes = info[rows_of(j), :]
        block_in, used_in = notes[:, 0:1], notes[:, 1:2]
        bits = chunk_of(shifts, j).astype(F32)
        shift_in = bits[:, 0:1] + bits[:, 1:2] + bits[:, 2:3]
        valid_in = iota((chunk_rows, BLK), 1).astype(F32) < used_in
        student = jnp.where(valid_in, jnp.exp(scores[rows_of(j), :] - shift_in), 0.0)
        spread[rows_of(j), :] = lift(student - teacher_n[rows_of(j), :], block_in)
        return carry

    lax.fori_loop(0, chunks, item_part, 0)

    def item_block(j, carry):
        columns = pl.ds(pl.multiple_of(j * 256, 256), 256)
        r["items_o"][columns, :] = tn(
            spread[:, columns], queries[...].reshape(rows, emb)
        )
        return carry

    lax.fori_loop(0, BLK_DEV * BLK // 256, item_block, 0)
    stores = [
        pltpu.make_async_copy(r[name + "_o"], r["grad_" + name], r["store_sem"].at[k])
        for k, name in enumerate(("items", "feats", "embed"))
    ]
    stores[0].start()
    for part in range(4):
        columns = pl.ds(part * (depth // 4), depth // 4)
        receive("gf" + str(part), "y", lambda p: gf_r.at[p, :, columns])
    gf_r[y] = gf_s[y]
    r["feats_o"][...] = jnp.sum(gf_r[...].astype(F32), axis=0)
    stores[1].start()
    receive("ex", "x", lambda p: ex.at[p])
    r["embed_o"][...] = ex[...].astype(F32).reshape(units, emb)
    stores[2].start()
    receive("zs", "z", lambda p: z_r.at[p])
    z_r[z] = jnp.zeros((half, units), BF16)
    r["grad_hidden"][...] = own + jnp.sum(z_r[...].astype(F32), axis=0)
    for store in stores:
        store.wait()
    for finish in pending:
        finish()


def hand_on(*refs):
    count = (len(refs) - 2) // 3
    sources, targets, buffers = refs[:count], refs[count : 2 * count], refs[2 * count : 3 * count]
    load_sem, store_sem = refs[-2:]
    loads = [
        pltpu.make_async_copy(sources[k], buffers[k], load_sem.at[k]) for k in range(count)
    ]
    stores = [
        pltpu.make_async_copy(buffers[k], targets[k], store_sem.at[k]) for k in range(count)
    ]
    for load in loads:
        load.start()
    for load, store in zip(loads, stores):
        load.wait()
        store.start()
    for store in stores:
        store.wait()


def per_device(
    n_z, n_x, n_y, feats, w_hidden, w_embed, items, teacher, block_counts, tail_rows,
    cand_owner, cand_block,
):
    q_dev, depth = feats.shape
    units, emb = w_embed.shape
    slots = cand_owner.shape[0]
    n_a, n_b = n_x * n_y, n_z * 2
    rows = n_a * n_b * CAP
    group_rows = n_y * q_dev
    block_cols = depth // (n_z * n_x)
    half = block_cols // 2
    part_units = units // n_x
    inputs = {
        "feats": feats,
        "w_hidden": w_hidden,
        "w_embed": w_embed,
        "items": items,
        "teacher": teacher,
        "counts": block_counts,
        "tails": tail_rows.reshape(1, q_dev),
        "owner": cand_owner.reshape(1, slots),
        "block": cand_block.reshape(1, slots),
    }
    outputs = {
        "grad_feats": (q_dev, depth),
        "grad_hidden": (half, units),
        "grad_embed": (units, emb),
        "grad_items": (BLK_DEV * BLK, emb),
    }
    vmem = {
        "weights": ((depth, units), BF16),
        "w_embed_v": ((units, emb), BF16),
        "items_v": ((BLK_DEV * BLK, emb), BF16),
        "items_o": ((BLK_DEV * BLK, emb), F32),
        "feats_o": ((q_dev, depth), F32),
        "embed_o": ((units, emb), F32),
        "feats_y": ((n_y, q_dev, depth), BF16),
        "perm": ((rows, rows), BF16),
        "member_row": ((rows, q_dev), F32),
        "preact": ((group_rows, units), F32),
        "preact_x": ((n_x, group_rows, units), BF16),
        "emb_s": ((n_y, q_dev, emb), F32),
        "emb_r": ((n_y, q_dev, emb), F32),
        "teacher_n": ((rows, BLK), F32),
        "info": ((rows, 128), F32),
        "spread": ((rows, BLK_DEV * BLK), BF16),
        "feats_s": ((n_x, group_rows, n_z * block_cols), BF16),
        "feats_x": ((n_x, group_rows, n_z * block_cols), BF16),
        "scores": ((rows, BLK), F32),
        "e1_q": ((n_b, 2 * n_a, 2 * BLK), BF16),
        "grad_a": ((n_a, q_dev, emb), BF16),
        "gf_s": ((n_y, q_dev, depth), BF16),
        "gf_r": ((n_y, q_dev, depth), BF16),
        "pre_x": ((n_x, group_rows, units), BF16),
        "halves": ((n_z, 2, half, units), F32),
        "halves_bf": ((n_z, 2, half, units), BF16),
        "core_r": ((n_z, half, units), BF16),
        "z_s": ((n_z, half, units), BF16),
        "z_r": ((n_z, half, units), BF16),
        "er_s": ((n_b, part_units // n_b, emb), BF16),
        "er_r": ((n_b, part_units // n_b, emb), BF16),
        "eb": ((n_b, part_units // n_b, emb), BF16),
        "ex": ((n_x, part_units, emb), BF16),
    }
    for name, lanes, ahead in (
        ("e1", 256, False),
        ("e2", emb, False),
        ("e3", emb, True),
        ("e4", emb + 128, False),
        ("e5", 128, True),
    ):
        one, two = ((n_a, 2 * n_b, lanes), (n_b, 2 * n_a, lanes))
        if not ahead:
            one, two = two, one
        for suffix, shape in (("_s1", one), ("_r1", one), ("_s2", two), ("_r2", two)):
            vmem[name + suffix] = (shape, BF16)
    scratch = [pltpu.VMEM(shape, kind) for shape, kind in vmem.values()]
    most = max(n_a, n_b)
    scratch += [
        pltpu.SemaphoreType.DMA((len(STAGES), most)),
        pltpu.SemaphoreType.DMA((len(STAGES), most)),
        pltpu.SemaphoreType.DMA((4,)),
        pltpu.SemaphoreType.DMA((3,)),
    ]
    names = list(inputs) + list(outputs) + list(vmem) + ["send_sem", "recv_sem", "load_sem", "store_sem"]
    large = ("feats", "w_hidden", "w_embed", "items")
    specs = [
        pl.BlockSpec(memory_space=pl.ANY if name in large else pltpu.VMEM)
        for name in inputs
    ]
    results = pl.pallas_call(
        functools.partial(kernel, n_z, n_x, n_y, names),
        out_shape=[jax.ShapeDtypeStruct(shape, F32) for shape in outputs.values()],
        in_specs=specs,
        out_specs=[
            pl.BlockSpec(memory_space=pltpu.VMEM if name == "grad_hidden" else pl.ANY)
            for name in outputs
        ],
        scratch_shapes=scratch,
        compiler_params=pltpu.CompilerParams(
            collective_id=0, has_side_effects=True, vmem_limit_bytes=58 * 1024 * 1024
        ),
    )(*inputs.values())
    return pl.pallas_call(
        hand_on,
        out_shape=[jax.ShapeDtypeStruct(shape, F32) for shape in outputs.values()],
        in_specs=[pl.BlockSpec(memory_space=pl.ANY)] * len(outputs),
        out_specs=[pl.BlockSpec(memory_space=pl.ANY)] * len(outputs),
        scratch_shapes=[pltpu.VMEM(shape, F32) for shape in outputs.values()]
        + [pltpu.SemaphoreType.DMA((len(outputs),))] * 2,
    )(*results)


def solution(mesh):
    n_y = mesh.shape["sub"]
    n_x = n_y
    n_z = mesh.shape["shard"] // (2 * n_x)
    both = ("shard", "sub")
    placed = (
        P(both, None),
        P(None, "sub"),
        P("sub", None),
        P(both, None),
        P(both, None),
        P(both, None),
        P(both),
        P(both, None),
        P(both),
    )
    return jax.shard_map(
        functools.partial(per_device, n_z, n_x, n_y),
        mesh=mesh,
        in_specs=placed,
        out_specs=(P(both, None), P("shard", "sub"), P("sub", None), P(both, None)),
        check_vma=False,
    )
```
